128 devices in a mesh: frame: 8 (over y, core), spatial: 2 (over x_lo), head: 8 (over x_hi, z).
Axes of the slice: x: 4 (x_hi: 2, x_lo: 2; x = x_hi * 2 + x_lo), y: 4, z: 4, core: 2. Of those that a mesh axis runs over, the one named last changes fastest.
Arguments:
- tokens: bfloat16 [16, 512, 3072], P('frame', 'spatial'), may hold values from -6 to 6
- w_qkv: bfloat16 [3072, 3, 3072], P(None, None, 'head'), may hold values from -0.109375 to 0.109375
- w_out: bfloat16 [3072, 3072], P('head'), may hold values from -0.109375 to 0.109375
- shift: float32 [3072], replicated, may hold values from -3 to 3
- scale: float32 [3072], replicated, may hold values from -2 to 2
- gate: float32 [3072], P('head'), may hold values from 0.5 to 1.5
- q_gain: float32 [128], replicated, may hold values from 1 to 2
- k_gain: float32 [128], replicated, may hold values from 1 to 2
- band: int32 [16], replicated, may hold values from 1 to 2
- far_tiles: int32 [16, 4, 4, 2], replicated, may hold values from 0 to 15, as said below
Outputs:
- update: bfloat16 [16, 512, 3072], P('frame', 'spatial', 'head')
The draws below stay inside these ranges and needn't reach their ends.
Inputs may be any that keep to these rules, and one draw needn't show every extreme that they name: `far_tiles`: A region is 2 consecutive frames starting at a multiple of 2, times the tiles 2 * s to 2 * s + 1 of each such frame; a block is 2 such frames. Every entry names a frame whose block differs from the query tile's block by 2 or more, counted cyclically over the 16 / 2 blocks, and a tile index below 4. The entries of all query tiles of one region name at most 2 distinct tiles of any one region, exactly 2 for some pair of regions. Entries of one query tile may repeat.
All inputs are finite; a program needn't handle non-finite values.
Results may differ from the reference program's by a relative error of at most 0.019.
Values may be sent and summed in bfloat16 or wider, within the bound.
No kernel may reach another device: no remote copies, remote signals or barrier semaphores. Data moves between devices by JAX's collectives and lax.ppermute only.
A program may use at most 128 MiB of HBM per device.

```python
import math
import jax
import jax.numpy as jnp
from jax import lax

D = 3072
HEADS = 24
HEAD_DIM = 128
FRAME_TOK = 512
FRAME_DEV = 2
TILE = 128
FAR = 4
CAP = 2
NFRAMES = 16
TILES_FRAME = 4
TILES_SP = 2
N_FRAME = 8
N_SPATIAL = 2


def draw_far_tiles(key, part):
    key = jax.random.fold_in(key, 11)
    subkeys = jax.random.split(key, 5)
    device_count = N_FRAME * N_SPATIAL
    local_count = FRAME_DEV * TILES_SP
    perm_keys = jax.random.split(subkeys[0], device_count * device_count)
    orders = jax.vmap(lambda one_key: jax.random.permutation(one_key, local_count))(perm_keys)
    orders = orders.reshape(device_count, device_count, local_count)[:, :, :CAP]
    grid_shape = (NFRAMES, TILES_FRAME, FAR)
    qframe = jnp.arange(NFRAMES, dtype=jnp.int32)[:, None, None]
    query_tile = jnp.arange(TILES_FRAME, dtype=jnp.int32)[None, :, None]
    entry_no = jnp.arange(FAR, dtype=jnp.int32)[None, None, :]
    qblock = qframe // FRAME_DEV
    query_owner = qblock * N_SPATIAL + query_tile // TILES_SP
    offset = jax.random.randint(subkeys[1], grid_shape, 0, N_FRAME - 3)
    half_pick = jax.random.randint(subkeys[2], grid_shape, 0, N_SPATIAL)
    slot_pick = jax.random.randint(subkeys[3], grid_shape, 0, CAP)
    chosen = jax.random.randint(subkeys[4], (), 0, NFRAMES * TILES_FRAME)
    flat_index = qframe * TILES_FRAME + query_tile
    is_chosen = (flat_index == chosen) & (entry_no < CAP)
    offset = jnp.where(is_chosen, offset[:, :, :1], offset)
    half_pick = jnp.where(is_chosen, half_pick[:, :, :1], half_pick)
    slot_pick = jnp.where(is_chosen, entry_no, slot_pick)
    source_block = (qblock + 2 + offset) % N_FRAME
    source_owner = source_block * N_SPATIAL + half_pick
    owner_full = jnp.broadcast_to(query_owner, grid_shape)
    local_tile = orders[owner_full, source_owner, slot_pick]
    far_frame = source_block * FRAME_DEV + local_tile // TILES_SP
    far_tile = half_pick * TILES_SP + local_tile % TILES_SP
    return jnp.stack([far_frame, far_tile], axis=-1).astype(jnp.int32)


def touch_ends(array, key, low, top_value):
    spot = [jax.random.randint(jax.random.fold_in(key, axis), (), 0, length) for axis, length in enumerate(array.shape)]
    main_axis = array.shape.index(max(array.shape))
    next_to = spot[:main_axis] + [(spot[main_axis] + 1) % array.shape[main_axis]] + spot[main_axis + 1:]
    return array.at[tuple(spot)].set(low).at[tuple(next_to)].set(top_value)


def level_of(key, shape, shards, low, top_value):
    level, own = 1.0, jax.random.fold_in(key, 6)
    for dim, blocks in shards:
        draws = jnp.exp(jax.random.uniform(jax.random.fold_in(own, dim), (blocks,), jnp.float32, low / len(shards), top_value / len(shards)))
        level = level * jnp.repeat(draws, shape[dim] // blocks).reshape([-1 if axis == dim else 1 for axis in range(len(shape))])
    return level


def noise(own_key, dims, deviation, limit, shards=(), kind=jnp.bfloat16):
    level = level_of(own_key, dims, shards, -0.22, 0.18) if shards else 1.0
    array = jax.random.normal(own_key, dims, jnp.float32) * deviation * level
    return jnp.minimum(jnp.maximum(array, -limit), limit).astype(kind)


def setup_inputs(seed: int = 0) -> dict:
    keys = jax.random.split(jax.random.key(seed), 11)
    return {
        "tokens": noise(keys[0], (NFRAMES, FRAME_TOK, D), 1.0, 6.0, ((0, 8), (1, 2))),
        "w_qkv": noise(keys[1], (D, 3, HEADS * HEAD_DIM), D ** -0.5, 0.109375, ((2, 8),)),
        "w_out": noise(keys[2], (HEADS * HEAD_DIM, D), (HEADS * HEAD_DIM) ** -0.5, 0.109375, ((0, 8),)),
        "shift": noise(keys[3], (D,), 0.5, 3.0, (), jnp.float32),
        "scale": noise(keys[4], (D,), 0.3, 2.0, (), jnp.float32),
        "gate": jnp.clip(0.5 + 1.0 * jax.random.uniform(keys[5], (D,), jnp.float32) ** level_of(keys[5], (D,), ((0, 8),), -0.2, 0.2), 0.5, 1.5),
        "q_gain": jnp.clip(jnp.exp(jax.random.uniform(keys[6], (HEAD_DIM,), jnp.float32, math.log(1.0), math.log(2.0))), 1.0, 2.0),
        "k_gain": jnp.clip(jnp.exp(jax.random.uniform(keys[7], (HEAD_DIM,), jnp.float32, math.log(1.0), math.log(2.0))), 1.0, 2.0),
        "band": touch_ends(jax.random.randint(keys[8], (NFRAMES,), 1, FRAME_DEV + 1), jax.random.fold_in(keys[8], 1), 1, FRAME_DEV).astype(jnp.int32),
        "far_tiles": draw_far_tiles(jax.random.fold_in(keys[10], 71), 0),
    }


NORM_EPS = 1e-06

def rms_norm(projected, gain):
    squares = lax.optimization_barrier(jnp.mean(projected * projected, axis=-1, keepdims=True))
    return (projected * lax.rsqrt(squares + NORM_EPS) * gain).astype(jnp.bfloat16)

def frame_mask(frame_no, band, far_tiles):
    key_frames = jnp.arange(NFRAMES, dtype=jnp.int32)
    key_tiles = jnp.arange(TILES_FRAME, dtype=jnp.int32)
    band_width = lax.dynamic_index_in_dim(band, frame_no, 0, keepdims=False)
    in_band = jnp.abs(key_frames - frame_no) <= band_width
    tile_lists = lax.dynamic_index_in_dim(far_tiles, frame_no, 0, keepdims=False)
    listed_hit = (tile_lists[:, :, 0][:, :, None, None] == key_frames[None, None, :, None]) & (tile_lists[:, :, 1][:, :, None, None] == key_tiles[None, None, None, :])
    listed = jnp.any(listed_hit, axis=1)
    allowed = (listed | in_band[None, :, None]).astype(jnp.float32)
    spread = jnp.broadcast_to(allowed[:, None, :, :, None], (TILES_FRAME, TILE, NFRAMES, TILES_FRAME, TILE))
    return spread.reshape(FRAME_TOK, NFRAMES * FRAME_TOK)

def reference(tokens, w_qkv, w_out, shift, scale, gate, q_gain, k_gain, band, far_tiles):
    row_count = NFRAMES * FRAME_TOK
    flat_rows = tokens.reshape(row_count, D).astype(jnp.float32)
    row_mean = lax.optimization_barrier(jnp.mean(flat_rows, axis=1, keepdims=True))
    centred = flat_rows - row_mean
    row_var = lax.optimization_barrier(jnp.mean(centred * centred, axis=1, keepdims=True))
    normed = (centred * lax.rsqrt(row_var + NORM_EPS) * (1.0 + scale) + shift).astype(jnp.bfloat16)
    projected = jnp.dot(normed, w_qkv.reshape(D, 3 * HEADS * HEAD_DIM), preferred_element_type=jnp.float32)
    projected = projected.reshape(row_count, 3, HEADS, HEAD_DIM)
    queries = rms_norm(projected[:, 0], q_gain)
    keys_normed = rms_norm(projected[:, 1], k_gain)
    values_bf = projected[:, 2].astype(jnp.bfloat16)
    query_frames = queries.reshape(NFRAMES, FRAME_TOK, HEADS, HEAD_DIM)
    key_heads = jnp.transpose(keys_normed, (1, 0, 2))
    value_heads = jnp.transpose(values_bf, (1, 0, 2))
    score_scale = HEAD_DIM ** (-0.5)

    def one_frame(frame_no):
        query_block = lax.dynamic_index_in_dim(query_frames, frame_no, 0, keepdims=False)
        key_mask = frame_mask(frame_no, band, far_tiles)

        def one_head(operands):
            query_one, key_one, value_one = operands
            scores = jnp.dot(query_one, key_one.T, preferred_element_type=jnp.float32) * score_scale
            weights = jnp.exp(scores) * key_mask
            denom_sum = lax.optimization_barrier(jnp.sum(weights, axis=1, keepdims=True))
            numer_sum = jnp.dot(weights.astype(jnp.bfloat16), value_one, preferred_element_type=jnp.float32)
            return (numer_sum / denom_sum).astype(jnp.bfloat16)
        return lax.map(one_head, (jnp.transpose(query_block, (1, 0, 2)), key_heads, value_heads))
    attended = lax.map(one_frame, jnp.arange(NFRAMES, dtype=jnp.int32))
    mixed_heads = jnp.transpose(attended, (0, 2, 1, 3)).reshape(row_count, HEADS * HEAD_DIM)
    result = jnp.dot(mixed_heads, w_out, preferred_element_type=jnp.float32) * gate
    return result.astype(jnp.bfloat16).reshape(NFRAMES, FRAME_TOK, D)
```

```python
import functools

import jax
import jax.numpy as jnp
from jax import lax
from jax.experimental import pallas as pl
from jax.experimental.pallas import tpu as pltpu
from jax.sharding import PartitionSpec as P

HEAD_DIM = 128
TILE = 128
NORM_EPS = 1e-06
LOG2E = 1.4426950408889634
ANY = pl.BlockSpec(memory_space=pl.ANY)
VMEM = pl.BlockSpec(memory_space=pltpu.VMEM)
SMEM = pl.BlockSpec(memory_space=pltpu.SMEM)
PARAMS = pltpu.CompilerParams(vmem_limit_bytes=56 * 1024 * 1024)
F32 = jnp.float32
BF16 = jnp.bfloat16


def rows_dot(a, b):
    return lax.dot_general(a, b, (((1,), (1,)), ((), ())), preferred_element_type=F32)


def rms_norm(part, gain):
    squares = jnp.mean(part * part, axis=-1, keepdims=True)
    return (part * lax.rsqrt(squares + NORM_EPS) * gain).astype(BF16)


def project_kernel(
    s_ref, x_ref, w_ref, scale_ref, shift_ref, qg_ref, kg_ref,
    ao_ref, am_ref, xkv_ref, ql_ref, qx_ref,
    x_scr, n_scr, w_scr, x_sem, w_sem,
):
    rows, width = n_scr.shape
    chunk = rows // 8
    x_copies = [
        pltpu.make_async_copy(
            x_ref.at[pl.ds(i * chunk, chunk)], x_scr.at[pl.ds(i * chunk, chunk)], x_sem.at[i]
        )
        for i in range(8)
    ]
    w_copies = [pltpu.make_async_copy(w_ref.at[j], w_scr.at[j], w_sem.at[j]) for j in range(3)]
    for copy in x_copies:
        copy.start()
    for j in (1, 2, 0):
        w_copies[j].start()
    gain = 1.0 + scale_ref[...]
    shift = shift_ref[...]
    for i in range(8):
        x_copies[i].wait()

        def one_block(step, carry, base=i * chunk):
            at = pl.ds(pl.multiple_of(base + step * 16, 16), 16)
            x = x_scr[at, :].astype(F32)
            centred = x - jnp.mean(x, axis=1, keepdims=True)
            var = jnp.mean(centred * centred, axis=1, keepdims=True)
            n_scr[at, :] = (centred * lax.rsqrt(var + NORM_EPS) * gain + shift).astype(BF16)
            return carry

        lax.fori_loop(0, chunk // 16, one_block, 0, unroll=True)
    first = s_ref[0] == 0
    kgain = kg_ref[...]
    qgain = qg_ref[...]

    def heads_of(j, gain_row):
        w_copies[j].wait()
        full = jnp.dot(n_scr[...], w_scr[j], preferred_element_type=F32)
        parts = [full[:, h * HEAD_DIM:(h + 1) * HEAD_DIM] for h in range(3)]
        if gain_row is None:
            parts = [part.astype(BF16) for part in parts]
        else:
            parts = [rms_norm(part, gain_row) for part in parts]
        own = jnp.where(first, parts[0], parts[2])
        other = jnp.where(first, parts[2], parts[0])
        shape = (2, rows // 2, HEAD_DIM)
        return own.reshape(shape), parts[1].reshape(shape), other.reshape(shape)

    for j, gain_row, low in ((1, kgain, 0), (2, None, HEAD_DIM)):
        own, mid, other = heads_of(j, gain_row)
        lanes = slice(low, low + HEAD_DIM)
        ao_ref[:, :, lanes] = own
        am_ref[:, :, lanes] = mid
        xkv_ref[:, :, lanes] = other
    own, mid, other = heads_of(0, qgain)
    ql_ref[:, :, :HEAD_DIM] = own
    ql_ref[:, :, HEAD_DIM:] = mid
    qx_ref[:, :, :HEAD_DIM] = other
    qx_ref[:, :, HEAD_DIM:] = mid


def project(s, tokens, w, scale, shift, q_gain, k_gain):
    frames, half_tok, width = tokens.shape
    rows = frames * half_tok
    piece = jax.ShapeDtypeStruct((frames, half_tok, 2 * HEAD_DIM), BF16)
    return pl.pallas_call(
        project_kernel,
        out_shape=[piece] * 5,
        in_specs=[SMEM, ANY, ANY] + [VMEM] * 4,
        out_specs=[VMEM] * 5,
        scratch_shapes=[
            pltpu.VMEM((rows, width), BF16),
            pltpu.VMEM((rows, width), BF16),
            pltpu.VMEM(w.shape, BF16),
            pltpu.SemaphoreType.DMA((8,)),
            pltpu.SemaphoreType.DMA((3,)),
        ],
        compiler_params=PARAMS,
        cost_estimate=pl.CostEstimate(
            flops=2 * rows * width * 9 * HEAD_DIM, bytes_accessed=12_000_000, transcendentals=0
        ),
        name="project",
    )(
        s.reshape(1), tokens.reshape(rows, width), w,
        scale.reshape(1, -1), shift.reshape(1, -1), q_gain.reshape(1, -1), k_gain.reshape(1, -1),
    )


META_BLOCKS = 1
META_FRAME = 9
META_BAND = 10
META_FAR = 12


def attend_kernel(meta_ref, *refs):
    ql_ref, qx_ref = refs[0:2]
    pieces = refs[2:26]
    home_ref, mid_ref, ret_ref = refs[26:29]
    q_scr, kvo, kvm, acc_o, acc_m, sem = refs[29:35]
    n_frames = kvo.shape[0]
    half = ql_ref.shape[1]
    s = meta_ref[0]
    copies = [
        pltpu.make_async_copy(ql_ref, q_scr.at[:, pl.ds(0, half)], sem.at[24]),
        pltpu.make_async_copy(qx_ref, q_scr.at[:, pl.ds(half, half)], sem.at[25]),
    ]
    two = pl.ds(0, 2 * HEAD_DIM)
    for r in range(8):
        frames = pl.ds(2 * meta_ref[META_BLOCKS + r], 2)
        near = pl.ds(pl.multiple_of(s * half, half), half)
        away = pl.ds(pl.multiple_of((1 - s) * half, half), half)
        copies.append(
            pltpu.make_async_copy(pieces[3 * r], kvo.at[frames, near, two], sem.at[3 * r])
        )
        copies.append(
            pltpu.make_async_copy(pieces[3 * r + 1], kvm.at[frames, :, two], sem.at[3 * r + 1])
        )
        copies.append(
            pltpu.make_async_copy(pieces[3 * r + 2], kvo.at[frames, away, two], sem.at[3 * r + 2])
        )
    for copy in copies:
        copy.start()
    ones = slice(2 * HEAD_DIM, 3 * HEAD_DIM)
    kvo[:, :, ones] = jnp.ones((n_frames, 2 * half, HEAD_DIM), BF16)
    kvm[:, :, ones] = jnp.ones((n_frames, half, HEAD_DIM), BF16)
    for copy in copies:
        copy.wait()
    factor = LOG2E * HEAD_DIM ** (-0.5)

    def weights_of(q, keys):
        return jnp.exp2(rows_dot(q, keys) * factor)

    eye = lax.broadcasted_iota(jnp.int32, (TILE, TILE), 0) == lax.broadcasted_iota(
        jnp.int32, (TILE, TILE), 1
    )
    first_frame = meta_ref[META_FRAME]
    for fi in range(2):
        frame = first_frame + fi
        width = meta_ref[META_BAND + fi]
        acc_o[...] = jnp.zeros_like(acc_o)
        acc_m[...] = jnp.zeros_like(acc_m)

        def one_frame(kf, carry, fi=fi):
            keys = kvo[kf]
            weights = weights_of(q_scr[fi, :, :HEAD_DIM], keys[:, :HEAD_DIM]).astype(BF16)
            acc_o[...] += jnp.dot(weights, keys[:, HEAD_DIM:], preferred_element_type=F32)
            keys = kvm[kf]
            weights = weights_of(q_scr[fi, :, HEAD_DIM:], keys[:, :HEAD_DIM]).astype(BF16)
            acc_m[...] += jnp.dot(weights, keys[:, HEAD_DIM:], preferred_element_type=F32)
            return carry

        low = jnp.maximum(frame - width, 0)
        high = jnp.minimum(frame + width, n_frames - 1)
        lax.fori_loop(low, high + 1, one_frame, 0)

        for r in range(2):
            for t in range(2):
                at = slice(r * half + t * TILE, r * half + (t + 1) * TILE)
                tile = 2 * (s ^ r) + t
                base = META_FAR + ((fi * 4 + tile) * 4) * 2
                entries = [(meta_ref[base + 2 * j], meta_ref[base + 2 * j + 1]) for j in range(4)]
                flags = []
                for j in range(4):
                    fresh = jnp.bool_(True)
                    for i in range(j):
                        same = (entries[i][0] == entries[j][0]) & (entries[i][1] == entries[j][1])
                        fresh = fresh & jnp.logical_not(same)
                    flags.append(fresh)
                keys = jnp.concatenate(
                    [kvo[kf, pl.ds(pl.multiple_of(kt * TILE, TILE), TILE), :] for kf, kt in entries],
                    axis=0,
                )
                weights = weights_of(q_scr[fi, at, :HEAD_DIM], keys[:, :HEAD_DIM])
                weights = jnp.concatenate(
                    [
                        weights[:, j * TILE:(j + 1) * TILE] * jnp.where(flags[j], 1.0, 0.0)
                        for j in range(4)
                    ],
                    axis=1,
                ).astype(BF16)
                acc_o[at, :] += jnp.dot(weights, keys[:, HEAD_DIM:], preferred_element_type=F32)
                keys = jnp.concatenate(
                    [
                        kvm[kf, pl.ds(pl.multiple_of((kt % 2) * TILE, TILE), TILE), :]
                        for kf, kt in entries
                    ],
                    axis=0,
                )
                weights = weights_of(q_scr[fi, at, HEAD_DIM:], keys[:, :HEAD_DIM])
                weights = jnp.concatenate(
                    [
                        weights[:, j * TILE:(j + 1) * TILE]
                        * jnp.where(flags[j] & (entries[j][1] // 2 == s), 1.0, 0.0)
                        for j in range(4)
                    ],
                    axis=1,
                ).astype(BF16)
                acc_m[at, :] += jnp.dot(weights, keys[:, HEAD_DIM:], preferred_element_type=F32)

        attended = (acc_o[:, :HEAD_DIM] / acc_o[:, HEAD_DIM:]).astype(BF16)
        home_ref[fi] = attended[:half]
        ret_ref[fi, :half, :HEAD_DIM] = attended[half:]
        mid_ref[fi] = acc_m[:half, :]
        ret_ref[fi, :half, HEAD_DIM:] = acc_m[half:, :HEAD_DIM].astype(BF16)
        dens = []
        for g in range(2):
            den = acc_m[half + g * TILE:half + (g + 1) * TILE, HEAD_DIM:]
            dens.append(jnp.sum(jnp.where(eye, den, 0.0), axis=0, keepdims=True))
        den = jnp.concatenate(dens, axis=0)
        upper = den.astype(BF16).astype(F32)
        block = jnp.concatenate([upper, den - upper, jnp.zeros((12, TILE), F32)], axis=0)
        ret_ref[fi, half:, :HEAD_DIM] = block.astype(BF16)
        ret_ref[fi, half:, HEAD_DIM:] = jnp.zeros((16, HEAD_DIM), BF16)


def attend(meta, q_home, q_away, pieces, n_frames):
    frames, half, _ = q_home.shape
    return pl.pallas_call(
        attend_kernel,
        out_shape=[
            jax.ShapeDtypeStruct((frames, half, HEAD_DIM), BF16),
            jax.ShapeDtypeStruct((frames, half, 2 * HEAD_DIM), F32),
            jax.ShapeDtypeStruct((frames, half + 16, 2 * HEAD_DIM), BF16),
        ],
        in_specs=[SMEM] + [ANY] * (2 + len(pieces)),
        out_specs=[VMEM] * 3,
        scratch_shapes=[
            pltpu.VMEM((frames, 2 * half, 2 * HEAD_DIM), BF16),
            pltpu.VMEM((n_frames, 2 * half, 3 * HEAD_DIM), BF16),
            pltpu.VMEM((n_frames, half, 3 * HEAD_DIM), BF16),
            pltpu.VMEM((2 * half, 2 * HEAD_DIM), F32),
            pltpu.VMEM((2 * half, 2 * HEAD_DIM), F32),
            pltpu.SemaphoreType.DMA((26,)),
        ],
        compiler_params=PARAMS,
        cost_estimate=pl.CostEstimate(
            flops=10_000_000_000, bytes_accessed=8_000_000, transcendentals=5_000_000
        ),
        name="attend",
    )(meta, q_home, q_away, *pieces)


def combine_kernel(s_ref, home_ref, mid_ref, got_ref, out0_ref, out1_ref):
    half = home_ref.shape[1]
    own_lanes = pl.ds(pl.multiple_of(s_ref[0] * 2 * HEAD_DIM, HEAD_DIM), HEAD_DIM)
    other_lanes = pl.ds(pl.multiple_of((1 - s_ref[0]) * 2 * HEAD_DIM, HEAD_DIM), HEAD_DIM)
    eye = lax.broadcasted_iota(jnp.int32, (TILE, TILE), 0) == lax.broadcasted_iota(
        jnp.int32, (TILE, TILE), 1
    )
    ones = jnp.ones((TILE, TILE), BF16)
    for fi, out_ref in enumerate((out0_ref, out1_ref)):
        out_ref[:, own_lanes] = home_ref[fi]
        out_ref[:, other_lanes] = got_ref[fi, :half, :HEAD_DIM]
        tail = got_ref[fi, half:, :HEAD_DIM].astype(F32)
        for g in range(2):
            at = slice(g * TILE, (g + 1) * TILE)
            upper = jnp.where(eye, tail[g:g + 1, :], 0.0).astype(BF16)
            lower = jnp.where(eye, tail[2 + g:3 + g, :], 0.0).astype(BF16)
            den = jnp.dot(upper, ones, preferred_element_type=F32) + jnp.dot(
                lower, ones, preferred_element_type=F32
            )
            num = mid_ref[fi, at, :HEAD_DIM] + got_ref[fi, at, HEAD_DIM:].astype(F32)
            out_ref[at, HEAD_DIM:2 * HEAD_DIM] = (
                num / (mid_ref[fi, at, HEAD_DIM:] + den)
            ).astype(BF16)


def combine(s, home, mid, got):
    half = home.shape[1]
    out = jax.ShapeDtypeStruct((half, 3 * HEAD_DIM), BF16)
    return pl.pallas_call(
        combine_kernel,
        out_shape=[out, out],
        in_specs=[SMEM, VMEM, VMEM, VMEM],
        out_specs=[VMEM, VMEM],
        compiler_params=PARAMS,
        cost_estimate=pl.CostEstimate(
            flops=50_000_000, bytes_accessed=1_500_000, transcendentals=0
        ),
        name="combine",
    )(s.reshape(1), home, mid, got)


def output_kernel(core_ref, *refs):
    mixed = refs[0:16]
    w_near, w_far = refs[16:20], refs[20:24]
    gate_ref, out_ref, h_scr, w_scr, h_sem, w_sem = refs[24:30]
    half, width = mixed[0].shape
    part = w_near[0].shape[1]
    core = core_ref[0]
    copies = []
    for k in range(4):
        for side in range(2):
            base = (side * 4 + k) * width
            for at, (source, which) in enumerate(((w_near, core), (w_far, 1 - core))):
                copies.append(
                    pltpu.make_async_copy(
                        source[k].at[side],
                        w_scr.at[pl.ds(pl.multiple_of(base + which * part, part), part)],
                        w_sem.at[(k * 2 + side) * 2 + at],
                    )
                )
    for fi in range(2):
        for g in range(8):
            copies.append(
                pltpu.make_async_copy(
                    mixed[fi * 8 + g],
                    h_scr.at[pl.ds(fi * half, half), pl.ds(g * width, width)],
                    h_sem.at[fi * 8 + g],
                )
            )
    for copy in copies:
        copy.start()
    for copy in copies:
        copy.wait()
    total = jnp.dot(h_scr[...], w_scr[...], preferred_element_type=F32)
    out_ref[...] = (total * gate_ref[...]).astype(BF16)


def output(core, mixed, w_near, w_far, gate):
    half, width = mixed[0].shape
    cols = w_near[0].shape[2]
    return pl.pallas_call(
        output_kernel,
        out_shape=jax.ShapeDtypeStruct((2 * half, cols), BF16),
        in_specs=[SMEM] + [ANY] * 24 + [VMEM],
        out_specs=VMEM,
        scratch_shapes=[
            pltpu.VMEM((2 * half, 8 * width), BF16),
            pltpu.VMEM((8 * width, cols), BF16),
            pltpu.SemaphoreType.DMA((16,)),
            pltpu.SemaphoreType.DMA((16,)),
        ],
        compiler_params=PARAMS,
        cost_estimate=pl.CostEstimate(
            flops=4 * half * 8 * width * cols, bytes_accessed=6_000_000, transcendentals=0
        ),
        name="output",
    )(core.reshape(1), *mixed, *w_near, *w_far, gate.reshape(1, -1))


def move(axis, to, x):
    count = lax.axis_size(axis)
    return lax.ppermute(x, axis, [(i, to(i)) for i in range(count)])


up_y = functools.partial(move, "frame", lambda i: (i + 2) % 8)
down_y = functools.partial(move, "frame", lambda i: (i + 6) % 8)
swap_core = functools.partial(move, "frame", lambda i: i ^ 1)
swap_half = functools.partial(move, "spatial", lambda i: i ^ 1)
up_z = functools.partial(move, "head", lambda i: i // 4 * 4 + (i + 1) % 4)
down_z = functools.partial(move, "head", lambda i: i // 4 * 4 + (i + 3) % 4)
cross_z = functools.partial(move, "head", lambda i: i // 4 * 4 + (i + 2) % 4)
swap_x = functools.partial(move, "head", lambda i: i ^ 4)


def ring(piece, up, down, by_up):
    before, after = up(piece), down(piece)
    return [piece, before, after, up(before) if by_up else down(after)]


def shards(tokens, w_qkv, w_out, shift, scale, gate, q_gain, k_gain, band, far_tiles):
    frames_dev, half_tok, model_width = tokens.shape
    n_frames = band.shape[0]
    f = lax.axis_index("frame")
    s = lax.axis_index("spatial")
    g = lax.axis_index("head")
    core, y, z, side = f % 2, f // 2, g % 4, g // 4

    part = w_out.shape[0] // 2
    cols = model_width // 8
    kept = lax.dynamic_slice(w_out, (core * part, side * 4 * cols), (part, 4 * cols))
    sent = lax.dynamic_slice(w_out, (core * part, (1 - side) * 4 * cols), (part, 4 * cols))
    both = jnp.stack([kept, swap_x(sent)])

    def w_for(step):
        return lax.dynamic_slice(both, (0, 0, (z + step) % 4 * cols), (2, part, cols))

    w_near = [w_for(0), up_z(w_for(1)), down_z(w_for(3)), cross_z(w_for(2))]
    w_far = [swap_core(w) for w in w_near]

    own, mid, other, q_home, q_send = project(
        s, tokens, jnp.transpose(w_qkv, (1, 0, 2)), scale, shift, q_gain, k_gain
    )
    away = swap_half(other)
    rings = [
        ring(own, up_y, down_y, True),
        ring(mid, up_y, down_y, False),
        ring(away, up_y, down_y, True),
    ]
    q_away = swap_half(q_send)
    pieces = []
    for r in range(4):
        pieces += [one[r] for one in rings]
    for r in range(4):
        pieces += [swap_core(one[r]) for one in rings]
    ys = jnp.stack([y, (y + 3) % 4, (y + 1) % 4, (y + 2) % 4])
    blocks = jnp.concatenate([2 * ys + core, 2 * ys + 1 - core])
    first = f * frames_dev
    meta = jnp.concatenate(
        [
            s.reshape(1),
            blocks,
            first.reshape(1),
            lax.dynamic_slice_in_dim(band, first, frames_dev, 0),
            lax.dynamic_slice_in_dim(far_tiles, first, frames_dev, 0).reshape(-1),
        ]
    ).astype(jnp.int32)
    home, mid_sums, back = attend(meta, q_home, q_away, pieces, n_frames)
    mixed = combine(s, home, mid_sums, swap_half(back))
    gathered = []
    for fi in range(2):
        gathered += ring(mixed[fi], up_z, down_z, fi == 0)
        gathered += ring(swap_x(mixed[fi]), up_z, down_z, fi == 0)
    result = output(core, gathered, w_near, w_far, gate)
    return result.reshape(frames_dev, half_tok, -1)


def solution(mesh):
    return jax.shard_map(
        shards,
        mesh=mesh,
        in_specs=(
            P("frame", "spatial", None),
            P(None, None, "head"),
            P("head", None),
            P(),
            P(),
            P("head"),
            P(),
            P(),
            P(),
            P(),
        ),
        out_specs=P("frame", "spatial", "head"),
        check_vma=False,
    )
```

```python
import functools

import jax
import jax.numpy as jnp
from jax import lax
from jax.experimental import pallas as pl
from jax.experimental.pallas import tpu as pltpu
from jax.sharding import PartitionSpec as P

HEAD_DIM = 128
TILE = 128
NORM_EPS = 1e-06
LOG2E = 1.4426950408889634
ANY = pl.BlockSpec(memory_space=pl.ANY)
VMEM = pl.BlockSpec(memory_space=pltpu.VMEM)
SMEM = pl.BlockSpec(memory_space=pltpu.SMEM)
PARAMS = pltpu.CompilerParams(vmem_limit_bytes=56 * 1024 * 1024)
F32 = jnp.float32
BF16 = jnp.bfloat16


def rows_dot(a, b):
    return lax.dot_general(a, b, (((1,), (1,)), ((), ())), preferred_element_type=F32)


def rms_norm(part, gain):
    squares = jnp.mean(part * part, axis=-1, keepdims=True)
    return (part * lax.rsqrt(squares + NORM_EPS) * gain).astype(BF16)


def split_heads(full, gain_row, first):
    parts = [full[:, h * HEAD_DIM:(h + 1) * HEAD_DIM] for h in range(3)]
    if gain_row is None:
        parts = [part.astype(BF16) for part in parts]
    else:
        parts = [rms_norm(part, gain_row) for part in parts]
    own = jnp.where(first, parts[0], parts[2])
    other = jnp.where(first, parts[2], parts[0])
    shape = (2, full.shape[0] // 2, HEAD_DIM)
    return own.reshape(shape), parts[1].reshape(shape), other.reshape(shape)


def project_kernel(
    place_ref, x_ref, w_ref, w_out_ref, scale_ref, shift_ref, qg_ref, kg_ref,
    kept_ref, sent_ref, home_ref, q_sent_ref, ahead_ref, apart_ref,
    n_scr, x_scr, w_scr, o_scr, x_sem, w_sem, o_sem,
):
    rows, width = x_scr.shape
    chunk = rows // 8
    x_copies = [
        pltpu.make_async_copy(
            x_ref.at[pl.ds(i * chunk, chunk)], x_scr.at[pl.ds(i * chunk, chunk)], x_sem.at[i]
        )
        for i in range(8)
    ]
    w_copies = [pltpu.make_async_copy(w_ref.at[j], w_scr.at[j], w_sem.at[j]) for j in range(3)]
    o_load = pltpu.make_async_copy(w_out_ref, o_scr, o_sem.at[0])
    for copy in x_copies + [w_copies[1], w_copies[2], w_copies[0], o_load]:
        copy.start()
    gain = 1.0 + scale_ref[...]
    shift = shift_ref[...]
    for i in range(8):
        x_copies[i].wait()

        def one_block(step, carry, base=i * chunk):
            at = pl.ds(pl.multiple_of(base + step * 16, 16), 16)
            x = x_scr[at, :].astype(F32)
            centred = x - jnp.mean(x, axis=1, keepdims=True)
            var = jnp.mean(centred * centred, axis=1, keepdims=True)
            n_scr[at, :] = (centred * lax.rsqrt(var + NORM_EPS) * gain + shift).astype(BF16)
            return carry

        lax.fori_loop(0, chunk // 16, one_block, 0, unroll=True)
    first = place_ref[0] == 0
    lanes = (slice(0, HEAD_DIM), slice(HEAD_DIM, 2 * HEAD_DIM), slice(2 * HEAD_DIM, 3 * HEAD_DIM),
             slice(3 * HEAD_DIM, 4 * HEAD_DIM))
    o_copies = []
    for j, gain_row in ((1, kg_ref[...]), (2, None), (0, qg_ref[...])):
        w_copies[j].wait()
        full = jnp.dot(n_scr[...], w_scr[j], preferred_element_type=F32)
        own, mid, other = split_heads(full, gain_row, first)
        if j == 0:
            home_ref[:, :, lanes[0]] = own
            home_ref[:, :, lanes[1]] = mid
            q_sent_ref[:, :, lanes[0]] = other
            q_sent_ref[:, :, lanes[1]] = mid
        else:
            kept_ref[:, :, lanes[j - 1]] = own
            kept_ref[:, :, lanes[j + 1]] = mid
            sent_ref[:, :, lanes[j - 1]] = other
        if j == 1:
            o_load.wait()
            cols, part = ahead_ref.shape[1] // 2, apart_ref.shape[0]
            for k in range(2):
                ahead = pl.ds(pl.multiple_of(place_ref[2 + k] * cols, TILE), cols)
                apart = pl.ds(pl.multiple_of(place_ref[4 + k] * cols, TILE), cols)
                half = pl.ds(pl.multiple_of(place_ref[1] * part, 16), part)
                to = pl.ds(k * cols, cols)
                o_copies += [
                    pltpu.make_async_copy(
                        o_scr.at[:, ahead], ahead_ref.at[:, to], o_sem.at[1 + 2 * k]
                    ),
                    pltpu.make_async_copy(
                        o_scr.at[half, apart], apart_ref.at[:, to], o_sem.at[2 + 2 * k]
                    ),
                ]
            for copy in o_copies:
                copy.start()
    for copy in o_copies:
        copy.wait()


def project(place, tokens, w, w_out, scale, shift, q_gain, k_gain):
    frames, half_tok, width = tokens.shape
    rows = frames * half_tok
    depth, cols = w_out.shape[0], w_out.shape[1] // 4
    piece = jax.ShapeDtypeStruct((frames, half_tok, 2 * HEAD_DIM), BF16)
    return pl.pallas_call(
        project_kernel,
        out_shape=[
            jax.ShapeDtypeStruct((frames, half_tok, 4 * HEAD_DIM), BF16),
            piece, piece, piece,
            jax.ShapeDtypeStruct((depth, cols), BF16),
            jax.ShapeDtypeStruct((depth // 2, cols), BF16),
        ],
        in_specs=[SMEM, ANY, ANY, ANY] + [VMEM] * 4,
        out_specs=[VMEM] * 4 + [ANY] * 2,
        scratch_shapes=[
            pltpu.VMEM((rows, width), BF16),
            pltpu.VMEM((rows, width), BF16),
            pltpu.VMEM(w.shape, BF16),
            pltpu.VMEM(w_out.shape, BF16),
            pltpu.SemaphoreType.DMA((8,)),
            pltpu.SemaphoreType.DMA((3,)),
            pltpu.SemaphoreType.DMA((5,)),
        ],
        compiler_params=PARAMS,
        cost_estimate=pl.CostEstimate(
            flops=2 * rows * width * 9 * HEAD_DIM, bytes_accessed=16_000_000, transcendentals=0
        ),
        name="project",
    )(
        place, tokens.reshape(rows, width), w, w_out,
        scale.reshape(1, -1), shift.reshape(1, -1), q_gain.reshape(1, -1), k_gain.reshape(1, -1),
    )


META_BLOCKS = 1
META_FRAME = 9
META_BAND = 10
META_FAR = 12
ONES = slice(2 * HEAD_DIM, 3 * HEAD_DIM)
FACTOR = LOG2E * HEAD_DIM ** (-0.5)


def weights_of(q, keys):
    return jnp.exp2(rows_dot(q, keys) * FACTOR)


def key_copies(meta_ref, blocks, pieces, kvo, kvm, sem):
    half = kvm.shape[1]
    s = meta_ref[0]
    near = pl.ds(pl.multiple_of(s * half, half), half)
    away = pl.ds(pl.multiple_of((1 - s) * half, half), half)
    two = pl.ds(0, 2 * HEAD_DIM)
    copies = []
    for at, block in enumerate(blocks):
        frames = pl.ds(2 * block, 2)
        kept, received = pieces[2 * at], pieces[2 * at + 1]
        copies += [
            pltpu.make_async_copy(kept.at[:, :, two], kvo.at[frames, near, two], sem.at[3 * at]),
            pltpu.make_async_copy(
                kept.at[:, :, pl.ds(2 * HEAD_DIM, 2 * HEAD_DIM)],
                kvm.at[frames, :, two],
                sem.at[3 * at + 1],
            ),
            pltpu.make_async_copy(received, kvo.at[frames, away, two], sem.at[3 * at + 2]),
        ]
    return copies


def query_copies(home_ref, away_ref, q_scr, sem, base):
    half = home_ref.shape[1]
    return [
        pltpu.make_async_copy(home_ref, q_scr.at[:, pl.ds(0, half)], sem.at[base]),
        pltpu.make_async_copy(away_ref, q_scr.at[:, pl.ds(half, half)], sem.at[base + 1]),
    ]


def add_frame(fi, at, q_scr, kvo, kvm, acc_o, acc_m):
    for lanes, kv, acc in (
        (slice(0, HEAD_DIM), kvo, acc_o),
        (slice(HEAD_DIM, 2 * HEAD_DIM), kvm, acc_m),
    ):
        keys = kv[at]
        weights = weights_of(q_scr[fi, :, lanes], keys[:, :HEAD_DIM]).astype(BF16)
        acc[fi] += jnp.dot(weights, keys[:, HEAD_DIM:], preferred_element_type=F32)


def near_kernel(meta_ref, home_ref, away_ref, *refs):
    pieces = refs[0:4]
    acc_o, acc_m, _, q_scr, kvo, kvm, sem = refs[5:12]
    local, half = kvm.shape[0], kvm.shape[1]
    start = meta_ref[META_FRAME] // local * local
    core = meta_ref[META_BLOCKS] % 2
    copies = query_copies(home_ref, away_ref, q_scr, sem, 6)
    copies += key_copies(meta_ref, [core, 1 - core], pieces, kvo, kvm, sem)
    for copy in copies:
        copy.start()
    kvo[:, :, ONES] = jnp.ones((local, 2 * half, HEAD_DIM), BF16)
    kvm[:, :, ONES] = jnp.ones((local, half, HEAD_DIM), BF16)
    acc_o[...] = jnp.zeros_like(acc_o)
    acc_m[...] = jnp.zeros_like(acc_m)
    for copy in copies:
        copy.wait()
    for fi in range(2):
        frame = meta_ref[META_FRAME] + fi - start
        width = meta_ref[META_BAND + fi]

        def one_frame(kf, carry, fi=fi):
            add_frame(fi, kf, q_scr, kvo, kvm, acc_o, acc_m)
            return carry

        lax.fori_loop(
            jnp.maximum(frame - width, 0), jnp.minimum(frame + width, local - 1) + 1, one_frame, 0
        )


def attend_near(meta, q_home, q_away, pieces, later):
    frames, half, _ = q_home.shape
    sums = jax.ShapeDtypeStruct((frames, 2 * half, 2 * HEAD_DIM), F32)
    return pl.pallas_call(
        near_kernel,
        out_shape=[sums, sums, jax.ShapeDtypeStruct(later.shape, later.dtype)],
        in_specs=[SMEM] + [ANY] * (3 + len(pieces)),
        out_specs=[VMEM] * 2 + [ANY],
        input_output_aliases={3 + len(pieces): 2},
        scratch_shapes=[
            pltpu.VMEM((frames, 2 * half, 2 * HEAD_DIM), BF16),
            pltpu.VMEM((2 * frames, 2 * half, 3 * HEAD_DIM), BF16),
            pltpu.VMEM((2 * frames, half, 3 * HEAD_DIM), BF16),
            pltpu.SemaphoreType.DMA((8,)),
        ],
        compiler_params=PARAMS,
        cost_estimate=pl.CostEstimate(
            flops=4_000_000_000, bytes_accessed=5_000_000, transcendentals=2_500_000
        ),
        name="attend_near",
    )(meta, q_home, q_away, *pieces, later)


def far_kernel(meta_ref, home_ref, away_ref, sums_o_ref, sums_m_ref, *refs):
    pieces = refs[0:12]
    out_ref, mid_ref, ret_ref = refs[16:19]
    q_scr, kvo, kvm, acc_o, acc_m, sem = refs[19:25]
    n_frames, half = kvm.shape[0], kvm.shape[1]
    s = meta_ref[0]
    copies = query_copies(home_ref, away_ref, q_scr, sem, 18)
    copies += [
        pltpu.make_async_copy(sums_o_ref, acc_o, sem.at[20]),
        pltpu.make_async_copy(sums_m_ref, acc_m, sem.at[21]),
    ]
    blocks = [meta_ref[META_BLOCKS + r] for r in range(2, 8)]
    copies += key_copies(meta_ref, blocks, pieces, kvo, kvm, sem)
    for copy in copies:
        copy.start()
    kvo[:, :, ONES] = jnp.ones((n_frames, 2 * half, HEAD_DIM), BF16)
    kvm[:, :, ONES] = jnp.ones((n_frames, half, HEAD_DIM), BF16)
    for copy in copies:
        copy.wait()
    eye = lax.broadcasted_iota(jnp.int32, (TILE, TILE), 0) == lax.broadcasted_iota(
        jnp.int32, (TILE, TILE), 1
    )
    start = meta_ref[META_FRAME] // 4 * 4
    for fi in range(2):
        frame = meta_ref[META_FRAME] + fi
        width = meta_ref[META_BAND + fi]

        def one_frame(kf, carry, fi=fi):
            add_frame(fi, kf, q_scr, kvo, kvm, acc_o, acc_m)
            return carry

        lax.fori_loop(jnp.maximum(frame - width, 0), start, one_frame, 0)
        lax.fori_loop(start + 4, jnp.minimum(frame + width, n_frames - 1) + 1, one_frame, 0)

        for r in range(2):
            for t in range(2):
                at = slice(r * half + t * TILE, r * half + (t + 1) * TILE)
                tile = 2 * (s ^ r) + t
                base = META_FAR + ((fi * 4 + tile) * 4) * 2
                entries = [(meta_ref[base + 2 * j], meta_ref[base + 2 * j + 1]) for j in range(4)]
                flags = []
                for j in range(4):
                    fresh = jnp.bool_(True)
                    for i in range(j):
                        same = (entries[i][0] == entries[j][0]) & (entries[i][1] == entries[j][1])
                        fresh = fresh & jnp.logical_not(same)
                    flags.append(fresh)
                mid_flags = [fresh & (entry[1] // 2 == s) for fresh, entry in zip(flags, entries)]
                for lanes, kv, acc, shown, tiles in (
                    (slice(0, HEAD_DIM), kvo, acc_o, flags, 4),
                    (slice(HEAD_DIM, 2 * HEAD_DIM), kvm, acc_m, mid_flags, 2),
                ):
                    keys = jnp.concatenate(
                        [
                            kv[kf, pl.ds(pl.multiple_of((kt % tiles) * TILE, TILE), TILE), :]
                            for kf, kt in entries
                        ],
                        axis=0,
                    )
                    weights = weights_of(q_scr[fi, at, lanes], keys[:, :HEAD_DIM])
                    weights = jnp.concatenate(
                        [
                            weights[:, j * TILE:(j + 1) * TILE] * jnp.where(shown[j], 1.0, 0.0)
                            for j in range(4)
                        ],
                        axis=1,
                    ).astype(BF16)
                    acc[fi, at, :] += jnp.dot(
                        weights, keys[:, HEAD_DIM:], preferred_element_type=F32
                    )

        attended = (acc_o[fi, :, :HEAD_DIM] / acc_o[fi, :, HEAD_DIM:]).astype(BF16)
        out_ref[fi] = attended[:half]
        ret_ref[fi, :half, :HEAD_DIM] = attended[half:]
        mid_ref[fi] = acc_m[fi, :half, :]
        ret_ref[fi, :half, HEAD_DIM:] = acc_m[fi, half:, :HEAD_DIM].astype(BF16)
        dens = []
        for g in range(2):
            den = acc_m[fi, half + g * TILE:half + (g + 1) * TILE, HEAD_DIM:]
            dens.append(jnp.sum(jnp.where(eye, den, 0.0), axis=0, keepdims=True))
        den = jnp.concatenate(dens, axis=0)
        upper = den.astype(BF16).astype(F32)
        block = jnp.concatenate([upper, den - upper, jnp.zeros((12, TILE), F32)], axis=0)
        ret_ref[fi, half:, :HEAD_DIM] = block.astype(BF16)
        ret_ref[fi, half:, HEAD_DIM:] = jnp.zeros((16, HEAD_DIM), BF16)


def attend_far(meta, q_home, q_away, sums, pieces, waited, n_frames):
    frames, half, _ = q_home.shape
    return pl.pallas_call(
        far_kernel,
        out_shape=[
            jax.ShapeDtypeStruct((frames, half, HEAD_DIM), BF16),
            jax.ShapeDtypeStruct((frames, half, 2 * HEAD_DIM), F32),
            jax.ShapeDtypeStruct((frames, half + 16, 2 * HEAD_DIM), BF16),
        ],
        in_specs=[SMEM] + [ANY] * (4 + len(pieces) + len(waited)),
        out_specs=[VMEM] * 3,
        scratch_shapes=[
            pltpu.VMEM((frames, 2 * half, 2 * HEAD_DIM), BF16),
            pltpu.VMEM((n_frames, 2 * half, 3 * HEAD_DIM), BF16),
            pltpu.VMEM((n_frames, half, 3 * HEAD_DIM), BF16),
            pltpu.VMEM((frames, 2 * half, 2 * HEAD_DIM), F32),
            pltpu.VMEM((frames, 2 * half, 2 * HEAD_DIM), F32),
            pltpu.SemaphoreType.DMA((22,)),
        ],
        compiler_params=PARAMS,
        cost_estimate=pl.CostEstimate(
            flops=5_000_000_000, bytes_accessed=10_000_000, transcendentals=2_500_000
        ),
        name="attend_far",
    )(meta, q_home, q_away, *sums, *pieces, *waited)


def combine_kernel(s_ref, home_ref, mid_ref, got_ref, out_ref):
    half = home_ref.shape[1]
    own_lanes = pl.ds(pl.multiple_of(s_ref[0] * 2 * HEAD_DIM, HEAD_DIM), HEAD_DIM)
    other_lanes = pl.ds(pl.multiple_of((1 - s_ref[0]) * 2 * HEAD_DIM, HEAD_DIM), HEAD_DIM)
    eye = lax.broadcasted_iota(jnp.int32, (TILE, TILE), 0) == lax.broadcasted_iota(
        jnp.int32, (TILE, TILE), 1
    )
    ones = jnp.ones((TILE, TILE), BF16)
    for fi in range(2):
        rows = pl.ds(fi * half, half)
        out_ref[rows, own_lanes] = home_ref[fi]
        out_ref[rows, other_lanes] = got_ref[fi, :half, :HEAD_DIM]
        tail = got_ref[fi, half:, :HEAD_DIM].astype(F32)
        for g in range(2):
            at = slice(g * TILE, (g + 1) * TILE)
            upper = jnp.where(eye, tail[g:g + 1, :], 0.0).astype(BF16)
            lower = jnp.where(eye, tail[2 + g:3 + g, :], 0.0).astype(BF16)
            den = jnp.dot(upper, ones, preferred_element_type=F32) + jnp.dot(
                lower, ones, preferred_element_type=F32
            )
            num = mid_ref[fi, at, :HEAD_DIM] + got_ref[fi, at, HEAD_DIM:].astype(F32)
            to = slice(fi * half + g * TILE, fi * half + (g + 1) * TILE)
            out_ref[to, HEAD_DIM:2 * HEAD_DIM] = (
                num / (mid_ref[fi, at, HEAD_DIM:] + den)
            ).astype(BF16)


def combine(s, home, mid, got):
    frames, half, _ = home.shape
    return pl.pallas_call(
        combine_kernel,
        out_shape=jax.ShapeDtypeStruct((frames * half, 3 * HEAD_DIM), BF16),
        in_specs=[SMEM, VMEM, VMEM, VMEM],
        out_specs=VMEM,
        compiler_params=PARAMS,
        cost_estimate=pl.CostEstimate(
            flops=50_000_000, bytes_accessed=1_500_000, transcendentals=0
        ),
        name="combine",
    )(s.reshape(1), home, mid, got)


def output_kernel(place_ref, *refs):
    mixed, (w_out_ref, ahead_ref, behind_ref, apart_ref, swapped_ref) = refs[0:4], refs[4:9]
    kept_ref, sent_ref, h_scr, w_scr, h_sem, w_sem = refs[9:15]
    width = mixed[0].shape[1]
    cols = kept_ref.shape[1]
    part = apart_ref.shape[0]
    core = place_ref[1]
    copies = []
    for k in range(4):
        at = pl.ds(k * width, width)
        copies.append(pltpu.make_async_copy(mixed[k], h_scr.at[:, at], h_sem.at[k]))
    for k in range(2):
        block = pl.ds(pl.multiple_of(place_ref[6 + k] * cols, TILE), cols)
        copies.append(
            pltpu.make_async_copy(
                w_out_ref.at[:, block],
                w_scr.at[pl.ds(0, width), pl.ds(k * cols, cols)],
                w_sem.at[k],
            )
        )
    for k, (source, base) in enumerate(
        (
            (ahead_ref, width),
            (behind_ref, 2 * width),
            (apart_ref, 3 * width + core * part),
            (swapped_ref, 3 * width + (1 - core) * part),
        )
    ):
        at = pl.ds(pl.multiple_of(base, 16), source.shape[0])
        copies.append(pltpu.make_async_copy(source, w_scr.at[at], w_sem.at[2 + k]))
    for copy in copies:
        copy.start()
    for copy in copies:
        copy.wait()
    sent_ref[...] = jnp.dot(
        h_scr[...], w_scr[:, cols:], preferred_element_type=F32
    ).astype(BF16)
    kept_ref[...] = jnp.dot(h_scr[...], w_scr[:, :cols], preferred_element_type=F32)


def output(place, mixed, w_out, weights):
    rows, width = mixed[0].shape
    cols = weights[0].shape[1] // 2
    return pl.pallas_call(
        output_kernel,
        out_shape=[
            jax.ShapeDtypeStruct((rows, cols), F32),
            jax.ShapeDtypeStruct((rows, cols), BF16),
        ],
        in_specs=[SMEM] + [ANY] * 9,
        out_specs=[VMEM] * 2,
        scratch_shapes=[
            pltpu.VMEM((rows, 4 * width), BF16),
            pltpu.VMEM((4 * width, 2 * cols), BF16),
            pltpu.SemaphoreType.DMA((4,)),
            pltpu.SemaphoreType.DMA((6,)),
        ],
        compiler_params=PARAMS,
        cost_estimate=pl.CostEstimate(
            flops=16 * rows * width * cols, bytes_accessed=6_000_000, transcendentals=0
        ),
        name="output",
    )(place, *mixed, w_out, *weights)


def move(axis, to, x):
    axes = axis if isinstance(axis, tuple) else (axis,)
    count = 1
    for name in axes:
        count *= lax.axis_size(name)
    return lax.ppermute(x, axis, [(i, to(i)) for i in range(count)])


def z_step(head, step):
    return head // 4 * 4 + (head + step) % 4


def z_by_core(step, i):
    frame, head = i // 8, i % 8
    return frame * 8 + z_step(head, step if frame % 2 == 0 else 4 - step)


swap_core = functools.partial(move, "frame", lambda i: i ^ 1)
out_y = functools.partial(move, "frame", lambda i: (i + (2 if i % 2 == 0 else 6)) % 8)
swap_half = functools.partial(move, "spatial", lambda i: i ^ 1)
cross_z = functools.partial(move, "head", lambda i: z_step(i, 2))
out_z = functools.partial(move, ("frame", "head"), functools.partial(z_by_core, 1))
in_z = functools.partial(move, ("frame", "head"), functools.partial(z_by_core, 3))
swap_x = functools.partial(move, "head", lambda i: i ^ 4)


def shards(tokens, w_qkv, w_out, shift, scale, gate, q_gain, k_gain, band, far_tiles):
    frames_dev, half_tok, model_width = tokens.shape
    n_frames = band.shape[0]
    f = lax.axis_index("frame")
    s = lax.axis_index("spatial")
    g = lax.axis_index("head")
    core, y, z, side = f % 2, f // 2, g % 4, g // 4

    step = jnp.where(core == 0, 1, 3)
    w = jnp.transpose(w_qkv, (1, 0, 2))
    columns = [(z + by) % 4 + 4 * to for by in (step, 2, 0) for to in (side, 1 - side)]
    place = jnp.stack([s, core] + columns)
    kept, sent, q_home, q_send, w_ahead, w_apart = project(
        place, tokens, w, w_out, scale, shift, q_gain, k_gain
    )
    q_away = swap_half(q_send)
    away = swap_half(sent)
    kept_other = swap_core(kept)
    kept_first, kept_second = out_y(kept), out_y(kept_other)
    away_other = swap_core(away)
    away_first, away_second = out_y(away), out_y(away_other)
    w_ahead, w_apart = out_z(w_ahead), cross_z(w_apart)
    w_parts = [w_ahead, swap_core(w_ahead), w_apart, swap_core(w_apart)]
    kept_across = out_y(kept_first)
    near_pieces = [kept, away, kept_other, away_other]
    ahead = (y + jnp.where(core == 0, 3, 1)) % 4
    behind = (y + jnp.where(core == 0, 1, 3)) % 4
    apart = (y + 2) % 4
    blocks = jnp.stack(
        [
            2 * y + core, 2 * y + 1 - core,
            2 * ahead + core, 2 * ahead + 1 - core,
            2 * behind + 1 - core, 2 * behind + core,
            2 * apart + core, 2 * apart + 1 - core,
        ]
    )
    start = f * frames_dev
    meta = jnp.concatenate(
        [
            s.reshape(1),
            blocks,
            start.reshape(1),
            lax.dynamic_slice_in_dim(band, start, frames_dev, 0),
            lax.dynamic_slice_in_dim(far_tiles, start, frames_dev, 0).reshape(-1),
        ]
    ).astype(jnp.int32)
    *sums, away_first = attend_near(meta, q_home, q_away, near_pieces, away_first)
    away_across = out_y(away_first)
    far = [
        (first, second, swap_core(first), swap_core(second), across, swap_core(across))
        for first, second, across in (
            (kept_first, kept_second, kept_across),
            (away_first, away_second, away_across),
        )
    ]
    far_pieces = [one[r] for r in range(6) for one in far]
    home, mid_sums, back = attend_far(
        meta, q_home, q_away, sums, far_pieces, w_parts, n_frames
    )
    mixed = combine(s, home, mid_sums, swap_half(back))
    ahead_z = out_z(mixed)
    gathered = [mixed, ahead_z, in_z(mixed), out_z(ahead_z)]
    kept_part, sent_part = output(place, gathered, w_out, w_parts)
    total = kept_part + swap_x(sent_part).astype(F32)
    return (total * gate).astype(BF16).reshape(frames_dev, half_tok, -1)


def solution(mesh):
    return jax.shard_map(
        shards,
        mesh=mesh,
        in_specs=(
            P("frame", "spatial", None),
            P(None, None, "head"),
            P("head", None),
            P(),
            P(),
            P("head"),
            P(),
            P(),
            P(),
            P(),
        ),
        out_specs=P("frame", "spatial", "head"),
        check_vma=False,
    )
```

```python
import functools

import jax
import jax.numpy as jnp
from jax import lax
from jax.experimental import pallas as pl
from jax.experimental.pallas import tpu as pltpu
from jax.sharding import PartitionSpec as P

HEAD_DIM = 128
TILE = 128
NORM_EPS = 1e-06
LOG2E = 1.4426950408889634
ANY = pl.BlockSpec(memory_space=pl.ANY)
HBM = pl.BlockSpec(memory_space=pltpu.HBM)
VMEM = pl.BlockSpec(memory_space=pltpu.VMEM)
SMEM = pl.BlockSpec(memory_space=pltpu.SMEM)
F32 = jnp.float32
BF16 = jnp.bfloat16


def vmem(mib):
    return pltpu.CompilerParams(vmem_limit_bytes=mib * 1024 * 1024)


def rows_dot(a, b):
    return lax.dot_general(a, b, (((1,), (1,)), ((), ())), preferred_element_type=F32)


def rms_norm(part, gain):
    squares = jnp.mean(part * part, axis=-1, keepdims=True)
    return (part * lax.rsqrt(squares + NORM_EPS) * gain).astype(BF16)


def split_heads(full, gain_row, first):
    parts = [full[:, h * HEAD_DIM:(h + 1) * HEAD_DIM] for h in range(3)]
    if gain_row is None:
        parts = [part.astype(BF16) for part in parts]
    else:
        parts = [rms_norm(part, gain_row) for part in parts]
    return jnp.where(first, parts[0], parts[2]), parts[1], jnp.where(first, parts[2], parts[0])


LANES = tuple(slice(k * HEAD_DIM, (k + 1) * HEAD_DIM) for k in range(4))
CHUNKS = 4


def project_kernel(
    place_ref, x_ref, w_ref, w_out_ref, scale_ref, shift_ref, qg_ref, kg_ref,
    kept_ref, sent_ref, home_ref, q_sent_ref, ahead_ref, apart_ref,
    n_scr, x_scr, w_scr, o_scr, kept_scr, sent_scr, home_scr, q_sent_scr,
    x_sem, w_sem, o_sem, out_sem,
):
    rows, width = x_scr.shape
    chunk = rows // CHUNKS
    wide = w_ref.shape[2]
    x_copies = [
        pltpu.make_async_copy(
            x_ref.at[pl.ds(i * chunk, chunk)], x_scr.at[pl.ds(i * chunk, chunk)], x_sem.at[i]
        )
        for i in range(CHUNKS)
    ]
    w_copies = [
        pltpu.make_async_copy(w_ref.at[j], w_scr.at[:, pl.ds(at * wide, wide)], w_sem.at[at])
        for at, j in enumerate((1, 2, 0))
    ]
    o_load = pltpu.make_async_copy(w_out_ref, o_scr, o_sem.at[0])
    for copy in x_copies + w_copies + [o_load]:
        copy.start()
    gain = 1.0 + scale_ref[...]
    shift = shift_ref[...]
    first = place_ref[0] == 0
    spans = [slice(i * chunk, (i + 1) * chunk) for i in range(CHUNKS)]

    def normalise(i):
        x_copies[i].wait()

        def one_block(step, carry):
            at = pl.ds(pl.multiple_of(i * chunk + step * 16, 16), 16)
            x = x_scr[at, :].astype(F32)
            centred = x - jnp.mean(x, axis=1, keepdims=True)
            var = jnp.mean(centred * centred, axis=1, keepdims=True)
            n_scr[at, :] = (centred * lax.rsqrt(var + NORM_EPS) * gain + shift).astype(BF16)
            return carry

        lax.fori_loop(0, chunk // 16, one_block, 0, unroll=True)

    normalise(0)
    w_copies[0].wait()
    w_copies[1].wait()
    for i, at in enumerate(spans):
        if i + 1 < CHUNKS:
            normalise(i + 1)
        full = jnp.dot(n_scr[at, :], w_scr[:, :2 * wide], preferred_element_type=F32)
        for j, gain_row in ((0, kg_ref[...]), (1, None)):
            own, mid, other = split_heads(full[:, j * wide:(j + 1) * wide], gain_row, first)
            kept_scr[at, LANES[j]] = own
            kept_scr[at, LANES[2 + j]] = mid
            sent_scr[at, LANES[j]] = other
    out_copies = [
        pltpu.make_async_copy(sent_scr, sent_ref, out_sem.at[0]),
        pltpu.make_async_copy(kept_scr, kept_ref, out_sem.at[1]),
        pltpu.make_async_copy(home_scr, home_ref, out_sem.at[2]),
        pltpu.make_async_copy(q_sent_scr, q_sent_ref, out_sem.at[3]),
    ]
    out_copies[0].start()
    out_copies[1].start()
    o_load.wait()
    cols, part = ahead_ref.shape[1] // 2, apart_ref.shape[0]
    half = pl.ds(pl.multiple_of(place_ref[1] * part, 16), part)
    o_copies = []
    for j in range(2):
        ahead = pl.ds(pl.multiple_of(place_ref[2 + j] * cols, TILE), cols)
        apart = pl.ds(pl.multiple_of(place_ref[4 + j] * cols, TILE), cols)
        to = pl.ds(j * cols, cols)
        o_copies += [
            pltpu.make_async_copy(o_scr.at[:, ahead], ahead_ref.at[:, to], o_sem.at[1 + 2 * j]),
            pltpu.make_async_copy(o_scr.at[half, apart], apart_ref.at[:, to], o_sem.at[2 + 2 * j]),
        ]
    for copy in o_copies:
        copy.start()
    w_copies[2].wait()
    for at in spans:
        full = jnp.dot(n_scr[at, :], w_scr[:, 2 * wide:], preferred_element_type=F32)
        own, mid, other = split_heads(full, qg_ref[...], first)
        home_scr[at, LANES[0]] = own
        home_scr[at, LANES[1]] = mid
        q_sent_scr[at, LANES[0]] = other
        q_sent_scr[at, LANES[1]] = mid
    out_copies[2].start()
    out_copies[3].start()
    for copy in out_copies + o_copies:
        copy.wait()


def project(place, tokens, w, w_out, scale, shift, q_gain, k_gain):
    frames, half_tok, width = tokens.shape
    rows = frames * half_tok
    shapes = [(rows, 4 * HEAD_DIM)] + [(rows, 2 * HEAD_DIM)] * 3
    depth, cols = w_out.shape[0], w_out.shape[1] // 4
    blocks = [(depth, cols), (depth // 2, cols)]
    pieces = pl.pallas_call(
        project_kernel,
        out_shape=[jax.ShapeDtypeStruct(shape, BF16) for shape in shapes + blocks],
        in_specs=[SMEM, ANY, ANY, ANY] + [VMEM] * 4,
        out_specs=[ANY] * 6,
        scratch_shapes=[
            pltpu.VMEM((rows, width), BF16),
            pltpu.VMEM((rows, width), BF16),
            pltpu.VMEM((width, 9 * HEAD_DIM), BF16),
            pltpu.VMEM(w_out.shape, BF16),
        ]
        + [pltpu.VMEM(shape, BF16) for shape in shapes]
        + [
            pltpu.SemaphoreType.DMA((CHUNKS,)),
            pltpu.SemaphoreType.DMA((3,)),
            pltpu.SemaphoreType.DMA((5,)),
            pltpu.SemaphoreType.DMA((4,)),
        ],
        compiler_params=vmem(56),
        cost_estimate=pl.CostEstimate(
            flops=2 * rows * width * 9 * HEAD_DIM, bytes_accessed=12_000_000, transcendentals=0
        ),
        name="project",
    )(
        place, tokens.reshape(rows, width), w, w_out,
        scale.reshape(1, -1), shift.reshape(1, -1), q_gain.reshape(1, -1), k_gain.reshape(1, -1),
    )
    return [piece.reshape(frames, half_tok, -1) for piece in pieces[:4]] + list(pieces[4:])


META_BLOCKS = 1
META_FRAME = 9
META_BAND = 10
META_FAR = 12
ONES = slice(2 * HEAD_DIM, 3 * HEAD_DIM)
FACTOR = LOG2E * HEAD_DIM ** (-0.5)


def weights_of(q, keys):
    return jnp.exp2(rows_dot(q, keys) * FACTOR)


def key_copies(meta_ref, blocks, pieces, kvo, kvm, sem):
    half = kvm.shape[1]
    s = meta_ref[0]
    near = pl.ds(pl.multiple_of(s * half, half), half)
    away = pl.ds(pl.multiple_of((1 - s) * half, half), half)
    two = pl.ds(0, 2 * HEAD_DIM)
    copies = []
    for at, block in enumerate(blocks):
        frames = pl.ds(2 * block, 2)
        kept, received = pieces[2 * at], pieces[2 * at + 1]
        copies += [
            pltpu.make_async_copy(kept.at[:, :, two], kvo.at[frames, near, two], sem.at[3 * at]),
            pltpu.make_async_copy(
                kept.at[:, :, pl.ds(2 * HEAD_DIM, 2 * HEAD_DIM)],
                kvm.at[frames, :, two],
                sem.at[3 * at + 1],
            ),
            pltpu.make_async_copy(received, kvo.at[frames, away, two], sem.at[3 * at + 2]),
        ]
    return copies


def query_copies(home_ref, away_ref, q_scr, sem, base):
    half = home_ref.shape[1]
    return [
        pltpu.make_async_copy(home_ref, q_scr.at[:, pl.ds(0, half)], sem.at[base]),
        pltpu.make_async_copy(away_ref, q_scr.at[:, pl.ds(half, half)], sem.at[base + 1]),
    ]


def add_frame(fi, at, q_scr, kvo, kvm, acc_o, acc_m):
    for lanes, kv, acc in (
        (slice(0, HEAD_DIM), kvo, acc_o),
        (slice(HEAD_DIM, 2 * HEAD_DIM), kvm, acc_m),
    ):
        keys = kv[at]
        weights = weights_of(q_scr[fi, :, lanes], keys[:, :HEAD_DIM]).astype(BF16)
        acc[fi] += jnp.dot(weights, keys[:, HEAD_DIM:], preferred_element_type=F32)


def attend_kernel(meta_ref, home_ref, away_ref, *refs):
    pieces = refs[0:16]
    out_ref, mid_ref, ret_ref = refs[18:21]
    q_scr, kvo, kvm, acc_o, acc_m, sem = refs[21:27]
    n_frames, half = kvm.shape[0], kvm.shape[1]
    s = meta_ref[0]
    moves = key_copies(
        meta_ref, [meta_ref[META_BLOCKS + r] for r in range(8)], pieces, kvo, kvm, sem
    )
    near = query_copies(home_ref, away_ref, q_scr, sem, 24) + moves[:6]
    band = moves[15:18]
    rest = moves[6:15] + moves[18:]
    for copy in near + band + rest:
        copy.start()
    kvo[:, :, ONES] = jnp.ones((n_frames, 2 * half, HEAD_DIM), BF16)
    kvm[:, :, ONES] = jnp.ones((n_frames, half, HEAD_DIM), BF16)
    acc_o[...] = jnp.zeros_like(acc_o)
    acc_m[...] = jnp.zeros_like(acc_m)
    eye = lax.broadcasted_iota(jnp.int32, (TILE, TILE), 0) == lax.broadcasted_iota(
        jnp.int32, (TILE, TILE), 1
    )
    start = meta_ref[META_FRAME] // 4 * 4

    def add_frames(fi, low, high):
        def one_frame(kf, carry):
            add_frame(fi, kf, q_scr, kvo, kvm, acc_o, acc_m)
            return carry

        lax.fori_loop(low, high + 1, one_frame, 0)

    spans = []
    for fi in range(2):
        frame = meta_ref[META_FRAME] + fi
        width = meta_ref[META_BAND + fi]
        spans.append((jnp.maximum(frame - width, 0), jnp.minimum(frame + width, n_frames - 1)))
    for copy in near:
        copy.wait()
    for fi, (low, high) in enumerate(spans):
        add_frames(fi, jnp.maximum(low, start), jnp.minimum(high, start + 3))
    for copy in band:
        copy.wait()
    for fi, (low, high) in enumerate(spans):
        add_frames(fi, low, start - 1)
        add_frames(fi, start + 4, high)
    for copy in rest:
        copy.wait()
    for fi in range(2):
        for r in range(2):
            for t in range(2):
                at = slice(r * half + t * TILE, r * half + (t + 1) * TILE)
                tile = 2 * (s ^ r) + t
                base = META_FAR + ((fi * 4 + tile) * 4) * 2
                entries = [(meta_ref[base + 2 * j], meta_ref[base + 2 * j + 1]) for j in range(4)]
                flags = []
                for j in range(4):
                    fresh = jnp.bool_(True)
                    for i in range(j):
                        same = (entries[i][0] == entries[j][0]) & (entries[i][1] == entries[j][1])
                        fresh = fresh & jnp.logical_not(same)
                    flags.append(fresh)
                mid_flags = [fresh & (entry[1] // 2 == s) for fresh, entry in zip(flags, entries)]
                for lanes, kv, acc, shown, tiles in (
                    (slice(0, HEAD_DIM), kvo, acc_o, flags, 4),
                    (slice(HEAD_DIM, 2 * HEAD_DIM), kvm, acc_m, mid_flags, 2),
                ):
                    keys = jnp.concatenate(
                        [
                            kv[kf, pl.ds(pl.multiple_of((kt % tiles) * TILE, TILE), TILE), :]
                            for kf, kt in entries
                        ],
                        axis=0,
                    )
                    weights = weights_of(q_scr[fi, at, lanes], keys[:, :HEAD_DIM])
                    weights = jnp.concatenate(
                        [
                            weights[:, j * TILE:(j + 1) * TILE] * jnp.where(shown[j], 1.0, 0.0)
                            for j in range(4)
                        ],
                        axis=1,
                    ).astype(BF16)
                    acc[fi, at, :] += jnp.dot(
                        weights, keys[:, HEAD_DIM:], preferred_element_type=F32
                    )

        attended = (acc_o[fi, :, :HEAD_DIM] / acc_o[fi, :, HEAD_DIM:]).astype(BF16)
        out_ref[fi * half:(fi + 1) * half, :] = attended[:half]
        ret_ref[fi, :half, :HEAD_DIM] = attended[half:]
        mid_ref[fi] = acc_m[fi, :half, :]
        ret_ref[fi, :half, HEAD_DIM:] = acc_m[fi, half:, :HEAD_DIM].astype(BF16)
        dens = []
        for g in range(2):
            den = acc_m[fi, half + g * TILE:half + (g + 1) * TILE, HEAD_DIM:]
            dens.append(jnp.sum(jnp.where(eye, den, 0.0), axis=0, keepdims=True))
        den = jnp.concatenate(dens, axis=0)
        upper = den.astype(BF16).astype(F32)
        block = jnp.concatenate([upper, den - upper, jnp.zeros((12, TILE), F32)], axis=0)
        ret_ref[fi, half:, :HEAD_DIM] = block.astype(BF16)
        ret_ref[fi, half:, HEAD_DIM:] = jnp.zeros((16, HEAD_DIM), BF16)


def attend(meta, q_home, q_away, pieces, waited, n_frames):
    frames, half, _ = q_home.shape
    return pl.pallas_call(
        attend_kernel,
        out_shape=[
            jax.ShapeDtypeStruct((frames * half, HEAD_DIM), BF16),
            jax.ShapeDtypeStruct((frames, half, 2 * HEAD_DIM), F32),
            jax.ShapeDtypeStruct((frames, half + 16, 2 * HEAD_DIM), BF16),
        ],
        in_specs=[SMEM, HBM, HBM]
        + [HBM if at in (0, 1, 3, 13, 15) else ANY for at in range(len(pieces))]
        + [ANY] * len(waited),
        out_specs=[VMEM] * 3,
        scratch_shapes=[
            pltpu.VMEM((frames, 2 * half, 2 * HEAD_DIM), BF16),
            pltpu.VMEM((n_frames, 2 * half, 3 * HEAD_DIM), BF16),
            pltpu.VMEM((n_frames, half, 3 * HEAD_DIM), BF16),
            pltpu.VMEM((frames, 2 * half, 2 * HEAD_DIM), F32),
            pltpu.VMEM((frames, 2 * half, 2 * HEAD_DIM), F32),
            pltpu.SemaphoreType.DMA((26,)),
        ],
        compiler_params=vmem(58),
        cost_estimate=pl.CostEstimate(
            flops=9_000_000_000, bytes_accessed=8_000_000, transcendentals=5_000_000
        ),
        name="attend",
    )(meta, q_home, q_away, *pieces, *waited)


def combine_kernel(place_ref, home_ref, mid_ref, got_ref, out0_ref, out1_ref, home, mid, got, sem):
    half = mid.shape[1]
    copies = [
        pltpu.make_async_copy(source, target, sem.at[k])
        for k, (source, target) in enumerate(
            ((got_ref, got), (mid_ref, mid), (home_ref, home))
        )
    ]
    for copy in copies:
        copy.start()
    s = place_ref[0]
    own_lanes = pl.ds(pl.multiple_of(s * 2 * HEAD_DIM, HEAD_DIM), HEAD_DIM)
    other_lanes = pl.ds(pl.multiple_of((1 - s) * 2 * HEAD_DIM, HEAD_DIM), HEAD_DIM)
    eye = lax.broadcasted_iota(jnp.int32, (TILE, TILE), 0) == lax.broadcasted_iota(
        jnp.int32, (TILE, TILE), 1
    )
    ones = jnp.ones((TILE, TILE), BF16)
    for copy in copies:
        copy.wait()
    for fi, out_ref in enumerate((out0_ref, out1_ref)):
        out_ref[:, own_lanes] = home[fi * half:(fi + 1) * half, :]
        out_ref[:, other_lanes] = got[fi, :half, :HEAD_DIM]
        tail = got[fi, half:, :HEAD_DIM].astype(F32)
        for g in range(2):
            at = slice(g * TILE, (g + 1) * TILE)
            upper = jnp.where(eye, tail[g:g + 1, :], 0.0).astype(BF16)
            lower = jnp.where(eye, tail[2 + g:3 + g, :], 0.0).astype(BF16)
            den = jnp.dot(upper, ones, preferred_element_type=F32) + jnp.dot(
                lower, ones, preferred_element_type=F32
            )
            num = mid[fi, at, :HEAD_DIM] + got[fi, at, HEAD_DIM:].astype(F32)
            out_ref[at, HEAD_DIM:2 * HEAD_DIM] = (num / (mid[fi, at, HEAD_DIM:] + den)).astype(BF16)


def combine(place, home, mid, got):
    frames, half, _ = mid.shape
    return pl.pallas_call(
        combine_kernel,
        out_shape=[jax.ShapeDtypeStruct((half, 3 * HEAD_DIM), BF16)] * frames,
        in_specs=[SMEM, ANY, ANY, ANY],
        out_specs=[VMEM] * frames,
        scratch_shapes=[
            pltpu.VMEM(home.shape, home.dtype),
            pltpu.VMEM(mid.shape, mid.dtype),
            pltpu.VMEM(got.shape, got.dtype),
            pltpu.SemaphoreType.DMA((3,)),
        ],
        compiler_params=vmem(6),
        cost_estimate=pl.CostEstimate(
            flops=50_000_000, bytes_accessed=1_500_000, transcendentals=0
        ),
        name="combine",
    )(place, home, mid, got)


def after_kernel(*refs):
    pass


def after(x, *waited):
    return pl.pallas_call(
        after_kernel,
        out_shape=jax.ShapeDtypeStruct(x.shape, x.dtype),
        in_specs=[ANY] * (1 + len(waited)),
        out_specs=ANY,
        input_output_aliases={0: 0},
        compiler_params=vmem(2),
        name="after",
    )(x, *waited)


def output_kernel(place_ref, *refs):
    mixed, w_out_ref = refs[0:4], refs[4]
    ahead_ref, behind_ref, apart_ref, swapped_ref = refs[5:9]
    kept_ref, sent_ref, h_scr, w_scr, h_sem, w_sem = refs[9:15]
    cols = kept_ref.shape[1]
    core = place_ref[1]
    width = mixed[0].shape[1]
    copies = [
        pltpu.make_async_copy(mixed[k], h_scr.at[:, pl.ds(k * width, width)], h_sem.at[k])
        for k in range(4)
    ]
    depth, part = ahead_ref.shape[0], apart_ref.shape[0]
    for j in range(2):
        block = pl.ds(pl.multiple_of(place_ref[6 + j] * cols, TILE), cols)
        copies.append(
            pltpu.make_async_copy(
                w_out_ref.at[:, block],
                w_scr.at[pl.ds(0, depth), pl.ds(j * cols, cols)],
                w_sem.at[j],
            )
        )
    for k, (source, base) in enumerate(
        (
            (ahead_ref, depth),
            (behind_ref, 2 * depth),
            (apart_ref, 3 * depth + core * part),
            (swapped_ref, 3 * depth + (1 - core) * part),
        )
    ):
        at = pl.ds(pl.multiple_of(base, 16), source.shape[0])
        copies.append(pltpu.make_async_copy(source, w_scr.at[at], w_sem.at[2 + k]))
    for copy in copies:
        copy.start()
    for copy in copies:
        copy.wait()
    sent_ref[...] = jnp.dot(
        h_scr[...], w_scr[:, cols:], preferred_element_type=F32
    ).astype(BF16)
    kept_ref[...] = jnp.dot(h_scr[...], w_scr[:, :cols], preferred_element_type=F32)


def output(place, mixed, w_out, w_parts):
    rows, width = mixed[0].shape
    cols = w_parts[0].shape[1] // 2
    return pl.pallas_call(
        output_kernel,
        out_shape=[
            jax.ShapeDtypeStruct((rows, cols), F32),
            jax.ShapeDtypeStruct((rows, cols), BF16),
        ],
        in_specs=[SMEM] + [ANY] * 9,
        out_specs=[VMEM] * 2,
        scratch_shapes=[
            pltpu.VMEM((rows, 4 * width), BF16),
            pltpu.VMEM((4 * width, 2 * cols), BF16),
            pltpu.SemaphoreType.DMA((4,)),
            pltpu.SemaphoreType.DMA((6,)),
        ],
        compiler_params=vmem(10),
        cost_estimate=pl.CostEstimate(
            flops=16 * rows * width * cols, bytes_accessed=4_000_000, transcendentals=0
        ),
        name="output",
    )(place, *mixed, w_out, *w_parts)


def move(axis, to, x):
    axes = axis if isinstance(axis, tuple) else (axis,)
    count = 1
    for name in axes:
        count *= lax.axis_size(name)
    return lax.ppermute(x, axis, [(i, to(i)) for i in range(count)])


def z_step(head, step):
    return head // 4 * 4 + (head + step) % 4


def z_by_core(step, i):
    frame, head = i // 8, i % 8
    return frame * 8 + z_step(head, step if frame % 2 == 0 else 4 - step)


swap_core = functools.partial(move, "frame", lambda i: i ^ 1)
out_y = functools.partial(move, "frame", lambda i: (i + (2 if i % 2 == 0 else 6)) % 8)
in_y = functools.partial(move, "frame", lambda i: (i + (6 if i % 2 == 0 else 2)) % 8)
cross_y = functools.partial(move, "frame", lambda i: (i + 4) % 8)
swap_half = functools.partial(move, "spatial", lambda i: i ^ 1)
cross_z = functools.partial(move, "head", lambda i: z_step(i, 2))
out_z = functools.partial(move, ("frame", "head"), functools.partial(z_by_core, 1))
in_z = functools.partial(move, ("frame", "head"), functools.partial(z_by_core, 3))
swap_x = functools.partial(move, "head", lambda i: i ^ 4)


def gather_z(x):
    return [x, out_z(x), in_z(x), cross_z(x)]


def shards(tokens, w_qkv, w_out, shift, scale, gate, q_gain, k_gain, band, far_tiles):
    frames_dev, half_tok, model_width = tokens.shape
    n_frames = band.shape[0]
    f = lax.axis_index("frame")
    s = lax.axis_index("spatial")
    g = lax.axis_index("head")
    core, y, z, side = f % 2, f // 2, g % 4, g // 4

    step = jnp.where(core == 0, 1, 3)
    w = jnp.transpose(w_qkv, (1, 0, 2))
    blocks_of_w = [(z + by) % 4 + 4 * to for by in (step, 2, 0) for to in (side, 1 - side)]
    place = jnp.stack([s, core] + blocks_of_w)
    kept, sent, q_home, q_send, w_ahead, w_apart = project(
        place, tokens, w, w_out, scale, shift, q_gain, k_gain
    )
    away = swap_half(sent)
    q_away = swap_half(q_send)
    kept_other, kept_first, kept_second = swap_core(kept), out_y(kept), in_y(kept)
    away_other, away_first, away_second = swap_core(away), out_y(away), in_y(away)
    away_across = cross_y(away)
    ahead = (y + jnp.where(core == 0, 3, 1)) % 4
    behind = (y + jnp.where(core == 0, 1, 3)) % 4
    apart = (y + 2) % 4
    blocks = jnp.stack(
        [
            2 * y + core, 2 * y + 1 - core,
            2 * ahead + core, 2 * behind + core,
            2 * behind + 1 - core, 2 * ahead + 1 - core,
            2 * apart + core, 2 * apart + 1 - core,
        ]
    )
    start = f * frames_dev
    meta = jnp.concatenate(
        [
            s.reshape(1),
            blocks,
            start.reshape(1),
            lax.dynamic_slice_in_dim(band, start, frames_dev, 0),
            lax.dynamic_slice_in_dim(far_tiles, start, frames_dev, 0).reshape(-1),
        ]
    ).astype(jnp.int32)
    kept_first = after(kept_first, kept_second)
    kept_across = out_y(kept_first)
    w_ahead, w_apart = out_z(w_ahead), cross_z(w_apart)
    pieces = [kept, away, kept_other, away_other]
    for kept_piece, away_piece in (
        (kept_first, away_first),
        (kept_second, away_second),
    ):
        pieces += [kept_piece, away_piece]
    for kept_piece, away_piece in (
        (kept_first, away_first),
        (kept_second, away_second),
    ):
        pieces += [swap_core(kept_piece), swap_core(away_piece)]
    pieces += [kept_across, away_across, swap_core(kept_across), swap_core(away_across)]
    home, mid_sums, back = attend(
        meta, q_home, q_away, pieces, [w_ahead, w_apart], n_frames
    )
    w_parts = [w_ahead, swap_core(w_ahead), w_apart, swap_core(w_apart)]
    totals = []
    for mixed in combine(place, home, mid_sums, swap_half(back)):
        kept_part, sent_part = output(place, gather_z(mixed), w_out, w_parts)
        totals.append(kept_part + swap_x(sent_part).astype(F32))
    return jnp.stack([(total * gate).astype(BF16) for total in totals])


def solution(mesh):
    return jax.shard_map(
        shards,
        mesh=mesh,
        in_specs=(
            P("frame", "spatial", None),
            P(None, None, "head"),
            P("head", None),
            P(),
            P(),
            P("head"),
            P(),
            P(),
            P(),
            P(),
        ),
        out_specs=P("frame", "spatial", "head"),
        check_vma=False,
    )
```

```python
import functools

import jax
import jax.numpy as jnp
from jax import lax
from jax.experimental import pallas as pl
from jax.experimental.pallas import tpu as pltpu
from jax.sharding import PartitionSpec as P

HEAD_DIM = 128
TILE = 128
NORM_EPS = 1e-06
LOG2E = 1.4426950408889634
ANY = pl.BlockSpec(memory_space=pl.ANY)
HBM = pl.BlockSpec(memory_space=pltpu.HBM)
VMEM = pl.BlockSpec(memory_space=pltpu.VMEM)
SMEM = pl.BlockSpec(memory_space=pltpu.SMEM)
F32 = jnp.float32
BF16 = jnp.bfloat16


def vmem(mib):
    return pltpu.CompilerParams(vmem_limit_bytes=mib * 1024 * 1024)


def rows_dot(a, b):
    return lax.dot_general(a, b, (((1,), (1,)), ((), ())), preferred_element_type=F32)


def rms_norm(part, gain):
    squares = jnp.mean(part * part, axis=-1, keepdims=True)
    return (part * lax.rsqrt(squares + NORM_EPS) * gain).astype(BF16)


def split_heads(full, gain_row, first):
    parts = [full[:, h * HEAD_DIM:(h + 1) * HEAD_DIM] for h in range(3)]
    if gain_row is None:
        parts = [part.astype(BF16) for part in parts]
    else:
        parts = [rms_norm(part, gain_row) for part in parts]
    return jnp.where(first, parts[0], parts[2]), parts[1], jnp.where(first, parts[2], parts[0])


LANES = tuple(slice(k * HEAD_DIM, (k + 1) * HEAD_DIM) for k in range(4))
CHUNKS = 4


def project_kernel(
    place_ref, x_ref, w_ref, w_out_ref, scale_ref, shift_ref, qg_ref, kg_ref,
    kept_ref, sent_ref, home_ref, q_sent_ref, ahead_ref, apart_ref,
    n_scr, x_scr, w_scr, o_scr, kept_scr, sent_scr, home_scr, q_sent_scr,
    x_sem, w_sem, o_sem, out_sem,
):
    rows, width = x_scr.shape
    chunk = rows // CHUNKS
    wide = w_ref.shape[2]
    x_copies = [
        pltpu.make_async_copy(
            x_ref.at[pl.ds(i * chunk, chunk)], x_scr.at[pl.ds(i * chunk, chunk)], x_sem.at[i]
        )
        for i in range(CHUNKS)
    ]
    w_copies = [
        pltpu.make_async_copy(w_ref.at[j], w_scr.at[:, pl.ds(at * wide, wide)], w_sem.at[at])
        for at, j in enumerate((1, 2, 0))
    ]
    o_load = pltpu.make_async_copy(w_out_ref, o_scr, o_sem.at[0])
    for copy in x_copies + w_copies[:1]:
        copy.start()
    gain = 1.0 + scale_ref[...]
    shift = shift_ref[...]
    first = place_ref[0] == 0
    spans = [slice(i * rows // 2, (i + 1) * rows // 2) for i in range(2)]

    def normalise(i):
        x_copies[i].wait()

        def one_block(step, carry):
            at = pl.ds(pl.multiple_of(i * chunk + step * 16, 16), 16)
            x = x_scr[at, :].astype(F32)
            centred = x - jnp.mean(x, axis=1, keepdims=True)
            var = jnp.mean(centred * centred, axis=1, keepdims=True)
            n_scr[at, :] = (centred * lax.rsqrt(var + NORM_EPS) * gain + shift).astype(BF16)
            return carry

        lax.fori_loop(0, chunk // 16, one_block, 0, unroll=True)

    for i in range(CHUNKS):
        if i == 1:
            for copy in w_copies[1:] + [o_load]:
                copy.start()
        normalise(i)
    w_copies[0].wait()
    w_copies[1].wait()
    for i, at in enumerate(spans):
        full = jnp.dot(n_scr[at, :], w_scr[:, :2 * wide], preferred_element_type=F32)
        for j, gain_row in ((0, kg_ref[...]), (1, None)):
            own, mid, other = split_heads(full[:, j * wide:(j + 1) * wide], gain_row, first)
            kept_scr[at, LANES[j]] = own
            kept_scr[at, LANES[2 + j]] = mid
            sent_scr[at, LANES[j]] = other
    out_copies = [
        pltpu.make_async_copy(sent_scr, sent_ref, out_sem.at[0]),
        pltpu.make_async_copy(kept_scr, kept_ref, out_sem.at[1]),
        pltpu.make_async_copy(home_scr, home_ref, out_sem.at[2]),
        pltpu.make_async_copy(q_sent_scr, q_sent_ref, out_sem.at[3]),
    ]
    out_copies[0].start()
    out_copies[1].start()
    o_load.wait()
    cols, part = ahead_ref.shape[1] // 2, apart_ref.shape[0]
    half = pl.ds(pl.multiple_of(place_ref[1] * part, 16), part)
    o_copies = []
    for j in range(2):
        ahead = pl.ds(pl.multiple_of(place_ref[2 + j] * cols, TILE), cols)
        apart = pl.ds(pl.multiple_of(place_ref[4 + j] * cols, TILE), cols)
        to = pl.ds(j * cols, cols)
        o_copies += [
            pltpu.make_async_copy(o_scr.at[:, ahead], ahead_ref.at[:, to], o_sem.at[1 + 2 * j]),
            pltpu.make_async_copy(o_scr.at[half, apart], apart_ref.at[:, to], o_sem.at[2 + 2 * j]),
        ]
    for copy in o_copies:
        copy.start()
    w_copies[2].wait()
    for at in spans:
        full = jnp.dot(n_scr[at, :], w_scr[:, 2 * wide:], preferred_element_type=F32)
        own, mid, other = split_heads(full, qg_ref[...], first)
        home_scr[at, LANES[0]] = own
        home_scr[at, LANES[1]] = mid
        q_sent_scr[at, LANES[0]] = other
        q_sent_scr[at, LANES[1]] = mid
    out_copies[2].start()
    out_copies[3].start()
    for copy in out_copies + o_copies:
        copy.wait()


def project(place, tokens, w, w_out, scale, shift, q_gain, k_gain):
    frames, half_tok, width = tokens.shape
    rows = frames * half_tok
    shapes = [(rows, 4 * HEAD_DIM)] + [(rows, 2 * HEAD_DIM)] * 3
    depth, cols = w_out.shape[0], w_out.shape[1] // 4
    blocks = [(depth, cols), (depth // 2, cols)]
    pieces = pl.pallas_call(
        project_kernel,
        out_shape=[jax.ShapeDtypeStruct(shape, BF16) for shape in shapes + blocks],
        in_specs=[SMEM, ANY, ANY, ANY] + [VMEM] * 4,
        out_specs=[ANY] * 6,
        scratch_shapes=[
            pltpu.VMEM((rows, width), BF16),
            pltpu.VMEM((rows, width), BF16),
            pltpu.VMEM((width, 9 * HEAD_DIM), BF16),
            pltpu.VMEM(w_out.shape, BF16),
        ]
        + [pltpu.VMEM(shape, BF16) for shape in shapes]
        + [
            pltpu.SemaphoreType.DMA((CHUNKS,)),
            pltpu.SemaphoreType.DMA((3,)),
            pltpu.SemaphoreType.DMA((5,)),
            pltpu.SemaphoreType.DMA((4,)),
        ],
        compiler_params=vmem(56),
        cost_estimate=pl.CostEstimate(
            flops=2 * rows * width * 9 * HEAD_DIM, bytes_accessed=12_000_000, transcendentals=0
        ),
        name="project",
    )(
        place, tokens.reshape(rows, width), w, w_out,
        scale.reshape(1, -1), shift.reshape(1, -1), q_gain.reshape(1, -1), k_gain.reshape(1, -1),
    )
    return [piece.reshape(frames, half_tok, -1) for piece in pieces[:4]] + list(pieces[4:])


META_BLOCKS = 1
META_FRAME = 9
META_BAND = 10
META_FAR = 12
ONES = slice(2 * HEAD_DIM, 3 * HEAD_DIM)
FACTOR = LOG2E * HEAD_DIM ** (-0.5)


def weights_of(q, keys):
    return jnp.exp2(rows_dot(q, keys) * FACTOR)


def key_copies(meta_ref, blocks, pieces, kvo, kvm, sem):
    half = kvm.shape[1]
    s = meta_ref[0]
    near = pl.ds(pl.multiple_of(s * half, half), half)
    away = pl.ds(pl.multiple_of((1 - s) * half, half), half)
    two = pl.ds(0, 2 * HEAD_DIM)
    copies = []
    for at, block in enumerate(blocks):
        frames = pl.ds(2 * block, 2)
        kept, received = pieces[2 * at], pieces[2 * at + 1]
        copies += [
            pltpu.make_async_copy(kept.at[:, :, two], kvo.at[frames, near, two], sem.at[3 * at]),
            pltpu.make_async_copy(
                kept.at[:, :, pl.ds(2 * HEAD_DIM, 2 * HEAD_DIM)],
                kvm.at[frames, :, two],
                sem.at[3 * at + 1],
            ),
            pltpu.make_async_copy(received, kvo.at[frames, away, two], sem.at[3 * at + 2]),
        ]
    return copies


def query_copies(home_ref, away_ref, q_scr, sem, base):
    half = home_ref.shape[1]
    return [
        pltpu.make_async_copy(home_ref, q_scr.at[:, pl.ds(0, half)], sem.at[base]),
        pltpu.make_async_copy(away_ref, q_scr.at[:, pl.ds(half, half)], sem.at[base + 1]),
    ]


def add_frame(fi, at, q_scr, kvo, kvm, acc_o, acc_m):
    for lanes, kv, acc in (
        (slice(0, HEAD_DIM), kvo, acc_o),
        (slice(HEAD_DIM, 2 * HEAD_DIM), kvm, acc_m),
    ):
        keys = kv[at]
        weights = weights_of(q_scr[fi, :, lanes], keys[:, :HEAD_DIM]).astype(BF16)
        acc[fi] += jnp.dot(weights, keys[:, HEAD_DIM:], preferred_element_type=F32)


def attend_kernel(meta_ref, home_ref, away_ref, *refs):
    pieces = refs[0:16]
    out_ref, mid_ref, ret_ref = refs[18:21]
    q_scr, kvo, kvm, acc_o, acc_m, sem = refs[21:27]
    n_frames, half = kvm.shape[0], kvm.shape[1]
    s = meta_ref[0]
    moves = key_copies(
        meta_ref, [meta_ref[META_BLOCKS + r] for r in range(8)], pieces, kvo, kvm, sem
    )
    near = query_copies(home_ref, away_ref, q_scr, sem, 24) + moves[:6]
    band = moves[15:18]
    rest = moves[6:15] + moves[18:]
    for copy in near + band + rest:
        copy.start()
    kvo[:, :, ONES] = jnp.ones((n_frames, 2 * half, HEAD_DIM), BF16)
    kvm[:, :, ONES] = jnp.ones((n_frames, half, HEAD_DIM), BF16)
    acc_o[...] = jnp.zeros_like(acc_o)
    acc_m[...] = jnp.zeros_like(acc_m)
    eye = lax.broadcasted_iota(jnp.int32, (TILE, TILE), 0) == lax.broadcasted_iota(
        jnp.int32, (TILE, TILE), 1
    )
    start = meta_ref[META_FRAME] // 4 * 4

    def add_frames(fi, low, high):
        def one_frame(kf, carry):
            add_frame(fi, kf, q_scr, kvo, kvm, acc_o, acc_m)
            return carry

        lax.fori_loop(low, high + 1, one_frame, 0)

    spans = []
    for fi in range(2):
        frame = meta_ref[META_FRAME] + fi
        width = meta_ref[META_BAND + fi]
        spans.append((jnp.maximum(frame - width, 0), jnp.minimum(frame + width, n_frames - 1)))
    for copy in near:
        copy.wait()
    for fi, (low, high) in enumerate(spans):
        add_frames(fi, jnp.maximum(low, start), jnp.minimum(high, start + 3))
    for copy in band:
        copy.wait()
    for fi, (low, high) in enumerate(spans):
        add_frames(fi, low, start - 1)
        add_frames(fi, start + 4, high)
    for copy in rest:
        copy.wait()
    for fi in range(2):
        for r in range(2):
            for t in range(2):
                at = slice(r * half + t * TILE, r * half + (t + 1) * TILE)
                tile = 2 * (s ^ r) + t
                base = META_FAR + ((fi * 4 + tile) * 4) * 2
                entries = [(meta_ref[base + 2 * j], meta_ref[base + 2 * j + 1]) for j in range(4)]
                flags = []
                for j in range(4):
                    fresh = jnp.bool_(True)
                    for i in range(j):
                        same = (entries[i][0] == entries[j][0]) & (entries[i][1] == entries[j][1])
                        fresh = fresh & jnp.logical_not(same)
                    flags.append(fresh)
                mid_flags = [fresh & (entry[1] // 2 == s) for fresh, entry in zip(flags, entries)]
                for lanes, kv, acc, shown, tiles in (
                    (slice(0, HEAD_DIM), kvo, acc_o, flags, 4),
                    (slice(HEAD_DIM, 2 * HEAD_DIM), kvm, acc_m, mid_flags, 2),
                ):
                    keys = jnp.concatenate(
                        [
                            kv[kf, pl.ds(pl.multiple_of((kt % tiles) * TILE, TILE), TILE), :]
                            for kf, kt in entries
                        ],
                        axis=0,
                    )
                    weights = weights_of(q_scr[fi, at, lanes], keys[:, :HEAD_DIM])
                    weights = jnp.concatenate(
                        [
                            weights[:, j * TILE:(j + 1) * TILE] * jnp.where(shown[j], 1.0, 0.0)
                            for j in range(4)
                        ],
                        axis=1,
                    ).astype(BF16)
                    acc[fi, at, :] += jnp.dot(
                        weights, keys[:, HEAD_DIM:], preferred_element_type=F32
                    )

        attended = (acc_o[fi, :, :HEAD_DIM] / acc_o[fi, :, HEAD_DIM:]).astype(BF16)
        out_ref[fi * half:(fi + 1) * half, :] = attended[:half]
        ret_ref[fi, :half, :HEAD_DIM] = attended[half:]
        mid_ref[fi] = acc_m[fi, :half, :]
        ret_ref[fi, :half, HEAD_DIM:] = acc_m[fi, half:, :HEAD_DIM].astype(BF16)
        dens = []
        for g in range(2):
            den = acc_m[fi, half + g * TILE:half + (g + 1) * TILE, HEAD_DIM:]
            dens.append(jnp.sum(jnp.where(eye, den, 0.0), axis=0, keepdims=True))
        den = jnp.concatenate(dens, axis=0)
        upper = den.astype(BF16).astype(F32)
        block = jnp.concatenate([upper, den - upper, jnp.zeros((12, TILE), F32)], axis=0)
        ret_ref[fi, half:, :HEAD_DIM] = block.astype(BF16)
        ret_ref[fi, half:, HEAD_DIM:] = jnp.zeros((16, HEAD_DIM), BF16)


def attend(meta, q_home, q_away, pieces, waited, n_frames):
    frames, half, _ = q_home.shape
    return pl.pallas_call(
        attend_kernel,
        out_shape=[
            jax.ShapeDtypeStruct((frames * half, HEAD_DIM), BF16),
            jax.ShapeDtypeStruct((frames, half, 2 * HEAD_DIM), F32),
            jax.ShapeDtypeStruct((frames, half + 16, 2 * HEAD_DIM), BF16),
        ],
        in_specs=[SMEM, HBM, HBM]
        + [HBM if at in (0, 1, 3, 13, 15) else ANY for at in range(len(pieces))]
        + [ANY] * len(waited),
        out_specs=[VMEM] * 3,
        scratch_shapes=[
            pltpu.VMEM((frames, 2 * half, 2 * HEAD_DIM), BF16),
            pltpu.VMEM((n_frames, 2 * half, 3 * HEAD_DIM), BF16),
            pltpu.VMEM((n_frames, half, 3 * HEAD_DIM), BF16),
            pltpu.VMEM((frames, 2 * half, 2 * HEAD_DIM), F32),
            pltpu.VMEM((frames, 2 * half, 2 * HEAD_DIM), F32),
            pltpu.SemaphoreType.DMA((26,)),
        ],
        compiler_params=vmem(58),
        cost_estimate=pl.CostEstimate(
            flops=9_000_000_000, bytes_accessed=8_000_000, transcendentals=5_000_000
        ),
        name="attend",
    )(meta, q_home, q_away, *pieces, *waited)


def combine_kernel(place_ref, home_ref, mid_ref, got_ref, _, out0_ref, out1_ref, home, mid, got, sem):
    half = mid.shape[1]
    copies = [
        pltpu.make_async_copy(source, target, sem.at[k])
        for k, (source, target) in enumerate(
            ((got_ref, got), (mid_ref, mid), (home_ref, home))
        )
    ]
    for copy in copies:
        copy.start()
    s = place_ref[0]
    own_lanes = pl.ds(pl.multiple_of(s * 2 * HEAD_DIM, HEAD_DIM), HEAD_DIM)
    other_lanes = pl.ds(pl.multiple_of((1 - s) * 2 * HEAD_DIM, HEAD_DIM), HEAD_DIM)
    eye = lax.broadcasted_iota(jnp.int32, (TILE, TILE), 0) == lax.broadcasted_iota(
        jnp.int32, (TILE, TILE), 1
    )
    ones = jnp.ones((TILE, TILE), BF16)
    for copy in copies:
        copy.wait()
    for fi, out_ref in enumerate((out0_ref, out1_ref)):
        out_ref[:, own_lanes] = home[fi * half:(fi + 1) * half, :]
        out_ref[:, other_lanes] = got[fi, :half, :HEAD_DIM]
        tail = got[fi, half:, :HEAD_DIM].astype(F32)
        for g in range(2):
            at = slice(g * TILE, (g + 1) * TILE)
            upper = jnp.where(eye, tail[g:g + 1, :], 0.0).astype(BF16)
            lower = jnp.where(eye, tail[2 + g:3 + g, :], 0.0).astype(BF16)
            den = jnp.dot(upper, ones, preferred_element_type=F32) + jnp.dot(
                lower, ones, preferred_element_type=F32
            )
            num = mid[fi, at, :HEAD_DIM] + got[fi, at, HEAD_DIM:].astype(F32)
            out_ref[at, HEAD_DIM:2 * HEAD_DIM] = (num / (mid[fi, at, HEAD_DIM:] + den)).astype(BF16)


def combine(place, home, mid, got, later):
    frames, half, _ = mid.shape
    return pl.pallas_call(
        combine_kernel,
        out_shape=[jax.ShapeDtypeStruct((half, 3 * HEAD_DIM), BF16)] * frames,
        in_specs=[SMEM, ANY, ANY, ANY, ANY],
        out_specs=[VMEM] * frames,
        scratch_shapes=[
            pltpu.VMEM(home.shape, home.dtype),
            pltpu.VMEM(mid.shape, mid.dtype),
            pltpu.VMEM(got.shape, got.dtype),
            pltpu.SemaphoreType.DMA((3,)),
        ],
        compiler_params=vmem(6),
        cost_estimate=pl.CostEstimate(
            flops=50_000_000, bytes_accessed=1_500_000, transcendentals=0
        ),
        name="combine",
    )(place, home, mid, got, later)


def after_kernel(*refs):
    pass


def after(x, *waited):
    return pl.pallas_call(
        after_kernel,
        out_shape=jax.ShapeDtypeStruct(x.shape, x.dtype),
        in_specs=[ANY] * (1 + len(waited)),
        out_specs=ANY,
        input_output_aliases={0: 0},
        compiler_params=vmem(2),
        name="after",
    )(x, *waited)


def assemble_kernel(place_ref, w_out_ref, ahead_ref, behind_ref, apart_ref, swapped_ref, *refs):
    all_ref, w_sem = refs[-2:]
    core = place_ref[1]
    depth, part = ahead_ref.shape[0], apart_ref.shape[0]
    cols = all_ref.shape[1] // 2
    copies = []
    for j in range(2):
        block = pl.ds(pl.multiple_of(place_ref[6 + j] * cols, TILE), cols)
        copies.append(
            pltpu.make_async_copy(
                w_out_ref.at[:, block],
                all_ref.at[pl.ds(0, depth), pl.ds(j * cols, cols)],
                w_sem.at[j],
            )
        )
    for k, (source, base) in enumerate(
        (
            (ahead_ref, depth),
            (behind_ref, 2 * depth),
            (apart_ref, 3 * depth + core * part),
            (swapped_ref, 3 * depth + (1 - core) * part),
        )
    ):
        at = pl.ds(pl.multiple_of(base, 16), source.shape[0])
        copies.append(pltpu.make_async_copy(source, all_ref.at[at], w_sem.at[2 + k]))
    for copy in copies:
        copy.start()
    for copy in copies:
        copy.wait()


def assemble(place, w_out, w_parts, later):
    depth, cols = w_parts[0].shape
    return pl.pallas_call(
        assemble_kernel,
        out_shape=jax.ShapeDtypeStruct((4 * depth, cols), BF16),
        in_specs=[SMEM] + [ANY] * 6,
        out_specs=VMEM,
        scratch_shapes=[pltpu.SemaphoreType.DMA((6,))],
        compiler_params=vmem(8),
        cost_estimate=pl.CostEstimate(flops=0, bytes_accessed=4_000_000, transcendentals=0),
        name="assemble",
    )(place, w_out, *w_parts, later)


def output_kernel(*refs):
    mixed, w_ref = refs[0:4], refs[4]
    kept_ref, sent_ref, h_scr, h_sem = refs[5:9]
    cols = kept_ref.shape[1]
    width = mixed[0].shape[1]
    copies = [
        pltpu.make_async_copy(mixed[k], h_scr.at[:, pl.ds(k * width, width)], h_sem.at[k])
        for k in range(4)
    ]
    for copy in copies:
        copy.start()
    for copy in copies:
        copy.wait()
    sent_ref[...] = jnp.dot(
        h_scr[...], w_ref[:, cols:], preferred_element_type=F32
    ).astype(BF16)
    kept_ref[...] = jnp.dot(h_scr[...], w_ref[:, :cols], preferred_element_type=F32)


def output(mixed, w_all):
    rows, width = mixed[0].shape
    cols = w_all.shape[1] // 2
    return pl.pallas_call(
        output_kernel,
        out_shape=[
            jax.ShapeDtypeStruct((rows, cols), F32),
            jax.ShapeDtypeStruct((rows, cols), BF16),
        ],
        in_specs=[ANY] * 4 + [VMEM],
        out_specs=[VMEM] * 2,
        scratch_shapes=[
            pltpu.VMEM((rows, 4 * width), BF16),
            pltpu.SemaphoreType.DMA((4,)),
        ],
        compiler_params=vmem(10),
        cost_estimate=pl.CostEstimate(
            flops=16 * rows * width * cols, bytes_accessed=4_000_000, transcendentals=0
        ),
        name="output",
    )(*mixed, w_all)


def move(axis, to, x):
    axes = axis if isinstance(axis, tuple) else (axis,)
    count = 1
    for name in axes:
        count *= lax.axis_size(name)
    return lax.ppermute(x, axis, [(i, to(i)) for i in range(count)])


def z_step(head, step):
    return head // 4 * 4 + (head + step) % 4


def z_by_core(step, i):
    frame, head = i // 8, i % 8
    return frame * 8 + z_step(head, step if frame % 2 == 0 else 4 - step)


swap_core = functools.partial(move, "frame", lambda i: i ^ 1)
out_y = functools.partial(move, "frame", lambda i: (i + (2 if i % 2 == 0 else 6)) % 8)
in_y = functools.partial(move, "frame", lambda i: (i + (6 if i % 2 == 0 else 2)) % 8)
cross_y = functools.partial(move, "frame", lambda i: (i + 4) % 8)
swap_half = functools.partial(move, "spatial", lambda i: i ^ 1)
cross_z = functools.partial(move, "head", lambda i: z_step(i, 2))
out_z = functools.partial(move, ("frame", "head"), functools.partial(z_by_core, 1))
in_z = functools.partial(move, ("frame", "head"), functools.partial(z_by_core, 3))
swap_x = functools.partial(move, "head", lambda i: i ^ 4)


def gather_z(x):
    ahead = out_z(x)
    return [x, ahead, in_z(x), out_z(ahead)]


def shards(tokens, w_qkv, w_out, shift, scale, gate, q_gain, k_gain, band, far_tiles):
    frames_dev, half_tok, model_width = tokens.shape
    n_frames = band.shape[0]
    f = lax.axis_index("frame")
    s = lax.axis_index("spatial")
    g = lax.axis_index("head")
    core, y, z, side = f % 2, f // 2, g % 4, g // 4

    step = jnp.where(core == 0, 1, 3)
    w = jnp.transpose(w_qkv, (1, 0, 2))
    blocks_of_w = [(z + by) % 4 + 4 * to for by in (step, 2, 0) for to in (side, 1 - side)]
    place = jnp.stack([s, core] + blocks_of_w)
    kept, sent, q_home, q_send, w_ahead, w_apart = project(
        place, tokens, w, w_out, scale, shift, q_gain, k_gain
    )
    away = swap_half(sent)
    q_away = swap_half(q_send)
    kept_other, kept_first, kept_second = swap_core(kept), out_y(kept), in_y(kept)
    away_other, away_first, away_second = swap_core(away), out_y(away), in_y(away)
    away_across = cross_y(away)
    ahead = (y + jnp.where(core == 0, 3, 1)) % 4
    behind = (y + jnp.where(core == 0, 1, 3)) % 4
    apart = (y + 2) % 4
    blocks = jnp.stack(
        [
            2 * y + core, 2 * y + 1 - core,
            2 * ahead + core, 2 * behind + core,
            2 * behind + 1 - core, 2 * ahead + 1 - core,
            2 * apart + core, 2 * apart + 1 - core,
        ]
    )
    start = f * frames_dev
    meta = jnp.concatenate(
        [
            s.reshape(1),
            blocks,
            start.reshape(1),
            lax.dynamic_slice_in_dim(band, start, frames_dev, 0),
            lax.dynamic_slice_in_dim(far_tiles, start, frames_dev, 0).reshape(-1),
        ]
    ).astype(jnp.int32)
    kept_first = after(kept_first, kept_second, meta)
    kept_across = out_y(kept_first)
    w_ahead, w_apart = out_z(w_ahead), cross_z(w_apart)
    pieces = [kept, away, kept_other, away_other]
    for kept_piece, away_piece in (
        (kept_first, away_first),
        (kept_second, away_second),
    ):
        pieces += [kept_piece, away_piece]
    for kept_piece, away_piece in (
        (kept_first, away_first),
        (kept_second, away_second),
    ):
        pieces += [swap_core(kept_piece), swap_core(away_piece)]
    pieces += [kept_across, away_across, swap_core(kept_across), swap_core(away_across)]
    home, mid_sums, back = attend(
        meta, q_home, q_away, pieces, [w_ahead, w_apart], n_frames
    )
    w_parts = [w_ahead, swap_core(w_ahead), w_apart, swap_core(w_apart)]
    totals = []
    w_all = assemble(place, w_out, w_parts, home)
    for mixed in combine(place, home, mid_sums, swap_half(back), w_all):
        kept_part, sent_part = output(gather_z(mixed), w_all)
        totals.append(kept_part + swap_x(sent_part).astype(F32))
    return jnp.stack([(total * gate).astype(BF16) for total in totals])


def solution(mesh):
    return jax.shard_map(
        shards,
        mesh=mesh,
        in_specs=(
            P("frame", "spatial", None),
            P(None, None, "head"),
            P("head", None),
            P(),
            P(),
            P("head"),
            P(),
            P(),
            P(),
            P(),
        ),
        out_specs=P("frame", "spatial", "head"),
        check_vma=False,
    )
```

```python
import functools

import jax
import jax.numpy as jnp
from jax import lax
from jax.experimental import pallas as pl
from jax.experimental.pallas import tpu as pltpu
from jax.sharding import PartitionSpec as P

HEAD_DIM = 128
TILE = 128
NORM_EPS = 1e-06
LOG2E = 1.4426950408889634
ANY = pl.BlockSpec(memory_space=pl.ANY)
HBM = pl.BlockSpec(memory_space=pltpu.HBM)
VMEM = pl.BlockSpec(memory_space=pltpu.VMEM)
SMEM = pl.BlockSpec(memory_space=pltpu.SMEM)
F32 = jnp.float32
BF16 = jnp.bfloat16


def vmem(mib):
    return pltpu.CompilerParams(vmem_limit_bytes=mib * 1024 * 1024)


def rows_dot(a, b):
    return lax.dot_general(a, b, (((1,), (1,)), ((), ())), preferred_element_type=F32)


def rms_norm(part, gain):
    squares = jnp.mean(part * part, axis=-1, keepdims=True)
    return (part * lax.rsqrt(squares + NORM_EPS) * gain).astype(BF16)


def split_heads(full, gain_row, first):
    parts = [full[:, h * HEAD_DIM:(h + 1) * HEAD_DIM] for h in range(3)]
    if gain_row is None:
        parts = [part.astype(BF16) for part in parts]
    else:
        parts = [rms_norm(part, gain_row) for part in parts]
    return jnp.where(first, parts[0], parts[2]), parts[1], jnp.where(first, parts[2], parts[0])


LANES = tuple(slice(k * HEAD_DIM, (k + 1) * HEAD_DIM) for k in range(4))
CHUNKS = 4


def project_kernel(
    place_ref, x_ref, w_ref, w_out_ref, scale_ref, shift_ref, qg_ref, kg_ref,
    kept_ref, sent_ref, home_ref, q_sent_ref, ahead_ref, apart_ref,
    n_scr, x_scr, w_scr, o_scr, kept_scr, sent_scr, home_scr, q_sent_scr,
    x_sem, w_sem, o_sem, out_sem,
):
    rows, width = x_scr.shape
    chunk = rows // CHUNKS
    wide = w_ref.shape[2]
    x_copies = [
        pltpu.make_async_copy(
            x_ref.at[pl.ds(i * chunk, chunk)], x_scr.at[pl.ds(i * chunk, chunk)], x_sem.at[i]
        )
        for i in range(CHUNKS)
    ]
    w_copies = [
        pltpu.make_async_copy(w_ref.at[j], w_scr.at[:, pl.ds(at * wide, wide)], w_sem.at[at])
        for at, j in enumerate((1, 2, 0))
    ]
    o_load = pltpu.make_async_copy(w_out_ref, o_scr, o_sem.at[0])
    for copy in x_copies + w_copies[:1]:
        copy.start()
    gain = 1.0 + scale_ref[...]
    shift = shift_ref[...]
    first = place_ref[0] == 0
    spans = [slice(i * rows // 2, (i + 1) * rows // 2) for i in range(2)]

    def normalise(i):
        x_copies[i].wait()

        def one_block(step, carry):
            at = pl.ds(pl.multiple_of(i * chunk + step * 16, 16), 16)
            x = x_scr[at, :].astype(F32)
            centred = x - jnp.mean(x, axis=1, keepdims=True)
            var = jnp.mean(centred * centred, axis=1, keepdims=True)
            n_scr[at, :] = (centred * lax.rsqrt(var + NORM_EPS) * gain + shift).astype(BF16)
            return carry

        lax.fori_loop(0, chunk // 16, one_block, 0, unroll=True)

    for i in range(CHUNKS):
        if i == 1:
            for copy in w_copies[1:] + [o_load]:
                copy.start()
        normalise(i)
    w_copies[0].wait()
    w_copies[1].wait()
    for i, at in enumerate(spans):
        full = jnp.dot(n_scr[at, :], w_scr[:, :2 * wide], preferred_element_type=F32)
        for j, gain_row in ((0, kg_ref[...]), (1, None)):
            own, mid, other = split_heads(full[:, j * wide:(j + 1) * wide], gain_row, first)
            kept_scr[at, LANES[j]] = own
            kept_scr[at, LANES[2 + j]] = mid
            sent_scr[at, LANES[j]] = other
    out_copies = [
        pltpu.make_async_copy(sent_scr, sent_ref, out_sem.at[0]),
        pltpu.make_async_copy(kept_scr, kept_ref, out_sem.at[1]),
        pltpu.make_async_copy(home_scr, home_ref, out_sem.at[2]),
        pltpu.make_async_copy(q_sent_scr, q_sent_ref, out_sem.at[3]),
    ]
    out_copies[0].start()
    out_copies[1].start()
    o_load.wait()
    cols, part = ahead_ref.shape[1] // 2, apart_ref.shape[0]
    half = pl.ds(pl.multiple_of(place_ref[1] * part, 16), part)
    o_copies = []
    for j in range(2):
        ahead = pl.ds(pl.multiple_of(place_ref[2 + j] * cols, TILE), cols)
        apart = pl.ds(pl.multiple_of(place_ref[4 + j] * cols, TILE), cols)
        to = pl.ds(j * cols, cols)
        o_copies += [
            pltpu.make_async_copy(o_scr.at[:, ahead], ahead_ref.at[:, to], o_sem.at[1 + 2 * j]),
            pltpu.make_async_copy(o_scr.at[half, apart], apart_ref.at[:, to], o_sem.at[2 + 2 * j]),
        ]
    for copy in o_copies:
        copy.start()
    w_copies[2].wait()
    for at in spans:
        full = jnp.dot(n_scr[at, :], w_scr[:, 2 * wide:], preferred_element_type=F32)
        own, mid, other = split_heads(full, qg_ref[...], first)
        home_scr[at, LANES[0]] = own
        home_scr[at, LANES[1]] = mid
        q_sent_scr[at, LANES[0]] = other
        q_sent_scr[at, LANES[1]] = mid
    out_copies[2].start()
    out_copies[3].start()
    for copy in out_copies + o_copies:
        copy.wait()


def project(place, tokens, w, w_out, scale, shift, q_gain, k_gain):
    frames, half_tok, width = tokens.shape
    rows = frames * half_tok
    shapes = [(rows, 4 * HEAD_DIM)] + [(rows, 2 * HEAD_DIM)] * 3
    depth, cols = w_out.shape[0], w_out.shape[1] // 4
    blocks = [(depth, cols), (depth // 2, cols)]
    pieces = pl.pallas_call(
        project_kernel,
        out_shape=[jax.ShapeDtypeStruct(shape, BF16) for shape in shapes + blocks],
        in_specs=[SMEM, ANY, ANY, ANY] + [VMEM] * 4,
        out_specs=[ANY] * 6,
        scratch_shapes=[
            pltpu.VMEM((rows, width), BF16),
            pltpu.VMEM((rows, width), BF16),
            pltpu.VMEM((width, 9 * HEAD_DIM), BF16),
            pltpu.VMEM(w_out.shape, BF16),
        ]
        + [pltpu.VMEM(shape, BF16) for shape in shapes]
        + [
            pltpu.SemaphoreType.DMA((CHUNKS,)),
            pltpu.SemaphoreType.DMA((3,)),
            pltpu.SemaphoreType.DMA((5,)),
            pltpu.SemaphoreType.DMA((4,)),
        ],
        compiler_params=vmem(56),
        cost_estimate=pl.CostEstimate(
            flops=2 * rows * width * 9 * HEAD_DIM, bytes_accessed=12_000_000, transcendentals=0
        ),
        name="project",
    )(
        place, tokens.reshape(rows, width), w, w_out,
        scale.reshape(1, -1), shift.reshape(1, -1), q_gain.reshape(1, -1), k_gain.reshape(1, -1),
    )
    return [piece.reshape(frames, half_tok, -1) for piece in pieces[:4]] + list(pieces[4:])


META_BLOCKS = 1
META_FRAME = 9
META_BAND = 10
META_FAR = 12
ONES = slice(2 * HEAD_DIM, 3 * HEAD_DIM)
FACTOR = LOG2E * HEAD_DIM ** (-0.5)


def weights_of(q, keys):
    return jnp.exp2(rows_dot(q, keys) * FACTOR)


def key_copies(meta_ref, blocks, pieces, kvo, kvm, sem):
    half = kvm.shape[1]
    s = meta_ref[0]
    near = pl.ds(pl.multiple_of(s * half, half), half)
    away = pl.ds(pl.multiple_of((1 - s) * half, half), half)
    two = pl.ds(0, 2 * HEAD_DIM)
    copies = []
    for at, block in enumerate(blocks):
        frames = pl.ds(2 * block, 2)
        kept, received = pieces[2 * at], pieces[2 * at + 1]
        copies += [
            pltpu.make_async_copy(kept.at[:, :, two], kvo.at[frames, near, two], sem.at[3 * at]),
            pltpu.make_async_copy(
                kept.at[:, :, pl.ds(2 * HEAD_DIM, 2 * HEAD_DIM)],
                kvm.at[frames, :, two],
                sem.at[3 * at + 1],
            ),
            pltpu.make_async_copy(received, kvo.at[frames, away, two], sem.at[3 * at + 2]),
        ]
    return copies


def query_copies(home_ref, away_ref, q_scr, sem, base):
    half = home_ref.shape[1]
    return [
        pltpu.make_async_copy(home_ref, q_scr.at[:, pl.ds(0, half)], sem.at[base]),
        pltpu.make_async_copy(away_ref, q_scr.at[:, pl.ds(half, half)], sem.at[base + 1]),
    ]


def add_frame(fi, at, q_scr, kvo, kvm, acc_o, acc_m):
    for lanes, kv, acc in (
        (slice(0, HEAD_DIM), kvo, acc_o),
        (slice(HEAD_DIM, 2 * HEAD_DIM), kvm, acc_m),
    ):
        keys = kv[at]
        weights = weights_of(q_scr[fi, :, lanes], keys[:, :HEAD_DIM]).astype(BF16)
        acc[fi] += jnp.dot(weights, keys[:, HEAD_DIM:], preferred_element_type=F32)


def attend_kernel(meta_ref, home_ref, away_ref, *refs):
    pieces = refs[0:16]
    out_ref, mid_ref, ret_ref = refs[18:21]
    q_scr, kvo, kvm, acc_o, acc_m, sem = refs[21:27]
    n_frames, half = kvm.shape[0], kvm.shape[1]
    s = meta_ref[0]
    moves = key_copies(
        meta_ref, [meta_ref[META_BLOCKS + r] for r in range(8)], pieces, kvo, kvm, sem
    )
    near = query_copies(home_ref, away_ref, q_scr, sem, 24) + moves[:6]
    band = moves[15:18]
    rest = moves[6:15] + moves[18:]
    for copy in near + band + rest:
        copy.start()
    kvo[:, :, ONES] = jnp.ones((n_frames, 2 * half, HEAD_DIM), BF16)
    kvm[:, :, ONES] = jnp.ones((n_frames, half, HEAD_DIM), BF16)
    acc_o[...] = jnp.zeros_like(acc_o)
    acc_m[...] = jnp.zeros_like(acc_m)
    eye = lax.broadcasted_iota(jnp.int32, (TILE, TILE), 0) == lax.broadcasted_iota(
        jnp.int32, (TILE, TILE), 1
    )
    start = meta_ref[META_FRAME] // 4 * 4

    def add_frames(fi, low, high):
        def one_frame(kf, carry):
            add_frame(fi, kf, q_scr, kvo, kvm, acc_o, acc_m)
            return carry

        lax.fori_loop(low, high + 1, one_frame, 0)

    spans = []
    for fi in range(2):
        frame = meta_ref[META_FRAME] + fi
        width = meta_ref[META_BAND + fi]
        spans.append((jnp.maximum(frame - width, 0), jnp.minimum(frame + width, n_frames - 1)))
    for copy in near:
        copy.wait()
    for fi, (low, high) in enumerate(spans):
        add_frames(fi, jnp.maximum(low, start), jnp.minimum(high, start + 3))
    for copy in band:
        copy.wait()
    for fi, (low, high) in enumerate(spans):
        add_frames(fi, low, start - 1)
        add_frames(fi, start + 4, high)
    for copy in rest:
        copy.wait()
    for fi in range(2):
        for r in range(2):
            for t in range(2):
                at = slice(r * half + t * TILE, r * half + (t + 1) * TILE)
                tile = 2 * (s ^ r) + t
                base = META_FAR + ((fi * 4 + tile) * 4) * 2
                entries = [(meta_ref[base + 2 * j], meta_ref[base + 2 * j + 1]) for j in range(4)]
                flags = []
                for j in range(4):
                    fresh = jnp.bool_(True)
                    for i in range(j):
                        same = (entries[i][0] == entries[j][0]) & (entries[i][1] == entries[j][1])
                        fresh = fresh & jnp.logical_not(same)
                    flags.append(fresh)
                mid_flags = [fresh & (entry[1] // 2 == s) for fresh, entry in zip(flags, entries)]
                for lanes, kv, acc, shown, tiles in (
                    (slice(0, HEAD_DIM), kvo, acc_o, flags, 4),
                    (slice(HEAD_DIM, 2 * HEAD_DIM), kvm, acc_m, mid_flags, 2),
                ):
                    keys = jnp.concatenate(
                        [
                            kv[kf, pl.ds(pl.multiple_of((kt % tiles) * TILE, TILE), TILE), :]
                            for kf, kt in entries
                        ],
                        axis=0,
                    )
                    weights = weights_of(q_scr[fi, at, lanes], keys[:, :HEAD_DIM])
                    weights = jnp.concatenate(
                        [
                            weights[:, j * TILE:(j + 1) * TILE] * jnp.where(shown[j], 1.0, 0.0)
                            for j in range(4)
                        ],
                        axis=1,
                    ).astype(BF16)
                    acc[fi, at, :] += jnp.dot(
                        weights, keys[:, HEAD_DIM:], preferred_element_type=F32
                    )

        attended = (acc_o[fi, :, :HEAD_DIM] / acc_o[fi, :, HEAD_DIM:]).astype(BF16)
        out_ref[fi * half:(fi + 1) * half, :] = attended[:half]
        ret_ref[fi, :half, :HEAD_DIM] = attended[half:]
        mid_ref[fi] = acc_m[fi, :half, :]
        ret_ref[fi, :half, HEAD_DIM:] = acc_m[fi, half:, :HEAD_DIM].astype(BF16)
        dens = []
        for g in range(2):
            den = acc_m[fi, half + g * TILE:half + (g + 1) * TILE, HEAD_DIM:]
            dens.append(jnp.sum(jnp.where(eye, den, 0.0), axis=0, keepdims=True))
        den = jnp.concatenate(dens, axis=0)
        upper = den.astype(BF16).astype(F32)
        block = jnp.concatenate([upper, den - upper, jnp.zeros((12, TILE), F32)], axis=0)
        ret_ref[fi, half:, :HEAD_DIM] = block.astype(BF16)
        ret_ref[fi, half:, HEAD_DIM:] = jnp.zeros((16, HEAD_DIM), BF16)


def attend(meta, q_home, q_away, pieces, waited, n_frames):
    frames, half, _ = q_home.shape
    return pl.pallas_call(
        attend_kernel,
        out_shape=[
            jax.ShapeDtypeStruct((frames * half, HEAD_DIM), BF16),
            jax.ShapeDtypeStruct((frames, half, 2 * HEAD_DIM), F32),
            jax.ShapeDtypeStruct((frames, half + 16, 2 * HEAD_DIM), BF16),
        ],
        in_specs=[SMEM, HBM, HBM]
        + [HBM if at in (0, 1, 3, 13, 15) else ANY for at in range(len(pieces))]
        + [ANY] * len(waited),
        out_specs=[VMEM] * 3,
        scratch_shapes=[
            pltpu.VMEM((frames, 2 * half, 2 * HEAD_DIM), BF16),
            pltpu.VMEM((n_frames, 2 * half, 3 * HEAD_DIM), BF16),
            pltpu.VMEM((n_frames, half, 3 * HEAD_DIM), BF16),
            pltpu.VMEM((frames, 2 * half, 2 * HEAD_DIM), F32),
            pltpu.VMEM((frames, 2 * half, 2 * HEAD_DIM), F32),
            pltpu.SemaphoreType.DMA((26,)),
        ],
        compiler_params=vmem(55),
        cost_estimate=pl.CostEstimate(
            flops=9_000_000_000, bytes_accessed=8_000_000, transcendentals=5_000_000
        ),
        name="attend",
    )(meta, q_home, q_away, *pieces, *waited)


def combine_kernel(place_ref, home_ref, mid_ref, got_ref, _, out0_ref, out1_ref, home, mid, got, sem):
    half = mid.shape[1]
    copies = [
        pltpu.make_async_copy(source, target, sem.at[k])
        for k, (source, target) in enumerate(
            ((got_ref, got), (mid_ref, mid), (home_ref, home))
        )
    ]
    for copy in copies:
        copy.start()
    s = place_ref[0]
    own_lanes = pl.ds(pl.multiple_of(s * 2 * HEAD_DIM, HEAD_DIM), HEAD_DIM)
    other_lanes = pl.ds(pl.multiple_of((1 - s) * 2 * HEAD_DIM, HEAD_DIM), HEAD_DIM)
    eye = lax.broadcasted_iota(jnp.int32, (TILE, TILE), 0) == lax.broadcasted_iota(
        jnp.int32, (TILE, TILE), 1
    )
    ones = jnp.ones((TILE, TILE), BF16)
    for copy in copies:
        copy.wait()
    for fi, out_ref in enumerate((out0_ref, out1_ref)):
        out_ref[:, own_lanes] = home[fi * half:(fi + 1) * half, :]
        out_ref[:, other_lanes] = got[fi, :half, :HEAD_DIM]
        tail = got[fi, half:, :HEAD_DIM].astype(F32)
        for g in range(2):
            at = slice(g * TILE, (g + 1) * TILE)
            upper = jnp.where(eye, tail[g:g + 1, :], 0.0).astype(BF16)
            lower = jnp.where(eye, tail[2 + g:3 + g, :], 0.0).astype(BF16)
            den = jnp.dot(upper, ones, preferred_element_type=F32) + jnp.dot(
                lower, ones, preferred_element_type=F32
            )
            num = mid[fi, at, :HEAD_DIM] + got[fi, at, HEAD_DIM:].astype(F32)
            out_ref[at, HEAD_DIM:2 * HEAD_DIM] = (num / (mid[fi, at, HEAD_DIM:] + den)).astype(BF16)


def combine(place, home, mid, got, later):
    frames, half, _ = mid.shape
    return pl.pallas_call(
        combine_kernel,
        out_shape=[jax.ShapeDtypeStruct((half, 3 * HEAD_DIM), BF16)] * frames,
        in_specs=[SMEM, ANY, ANY, ANY, ANY],
        out_specs=[VMEM] * frames,
        scratch_shapes=[
            pltpu.VMEM(home.shape, home.dtype),
            pltpu.VMEM(mid.shape, mid.dtype),
            pltpu.VMEM(got.shape, got.dtype),
            pltpu.SemaphoreType.DMA((3,)),
        ],
        compiler_params=vmem(6),
        cost_estimate=pl.CostEstimate(
            flops=50_000_000, bytes_accessed=1_500_000, transcendentals=0
        ),
        name="combine",
    )(place, home, mid, got, later)


def after_kernel(*refs):
    pass


def after(x, *waited):
    return pl.pallas_call(
        after_kernel,
        out_shape=jax.ShapeDtypeStruct(x.shape, x.dtype),
        in_specs=[ANY] * (1 + len(waited)),
        out_specs=ANY,
        input_output_aliases={0: 0},
        compiler_params=vmem(2),
        name="after",
    )(x, *waited)


def assemble_kernel(place_ref, w_out_ref, ahead_ref, behind_ref, apart_ref, swapped_ref, *refs):
    all_ref, w_sem = refs[-2:]
    core = place_ref[1]
    depth, part = ahead_ref.shape[0], apart_ref.shape[0]
    cols = all_ref.shape[1] // 2
    copies = []
    for j in range(2):
        block = pl.ds(pl.multiple_of(place_ref[6 + j] * cols, TILE), cols)
        copies.append(
            pltpu.make_async_copy(
                w_out_ref.at[:, block],
                all_ref.at[pl.ds(0, depth), pl.ds(j * cols, cols)],
                w_sem.at[j],
            )
        )
    for k, (source, base) in enumerate(
        (
            (ahead_ref, depth),
            (behind_ref, 2 * depth),
            (apart_ref, 3 * depth + core * part),
            (swapped_ref, 3 * depth + (1 - core) * part),
        )
    ):
        at = pl.ds(pl.multiple_of(base, 16), source.shape[0])
        copies.append(pltpu.make_async_copy(source, all_ref.at[at], w_sem.at[2 + k]))
    for copy in copies:
        copy.start()
    for copy in copies:
        copy.wait()


def assemble(place, w_out, w_parts, later):
    depth, cols = w_parts[0].shape
    return pl.pallas_call(
        assemble_kernel,
        out_shape=jax.ShapeDtypeStruct((4 * depth, cols), BF16),
        in_specs=[SMEM] + [ANY] * 6,
        out_specs=VMEM,
        scratch_shapes=[pltpu.SemaphoreType.DMA((6,))],
        compiler_params=vmem(8),
        cost_estimate=pl.CostEstimate(flops=0, bytes_accessed=4_000_000, transcendentals=0),
        name="assemble",
    )(place, w_out, *w_parts, later)


def output_kernel(*refs):
    mixed, w_ref = refs[0:4], refs[4]
    kept_ref, sent_ref, h_scr, h_sem = refs[5:9]
    cols = kept_ref.shape[1]
    width = mixed[0].shape[1]
    copies = [
        pltpu.make_async_copy(mixed[k], h_scr.at[:, pl.ds(k * width, width)], h_sem.at[k])
        for k in range(4)
    ]
    for copy in copies:
        copy.start()
    for copy in copies:
        copy.wait()
    sent_ref[...] = jnp.dot(
        h_scr[...], w_ref[:, cols:], preferred_element_type=F32
    ).astype(BF16)
    kept_ref[...] = jnp.dot(h_scr[...], w_ref[:, :cols], preferred_element_type=F32)


def output(mixed, w_all):
    rows, width = mixed[0].shape
    cols = w_all.shape[1] // 2
    return pl.pallas_call(
        output_kernel,
        out_shape=[
            jax.ShapeDtypeStruct((rows, cols), F32),
            jax.ShapeDtypeStruct((rows, cols), BF16),
        ],
        in_specs=[ANY] * 4 + [VMEM],
        out_specs=[VMEM] * 2,
        scratch_shapes=[
            pltpu.VMEM((rows, 4 * width), BF16),
            pltpu.SemaphoreType.DMA((4,)),
        ],
        compiler_params=vmem(10),
        cost_estimate=pl.CostEstimate(
            flops=16 * rows * width * cols, bytes_accessed=4_000_000, transcendentals=0
        ),
        name="output",
    )(*mixed, w_all)


def move(axis, to, x):
    axes = axis if isinstance(axis, tuple) else (axis,)
    count = 1
    for name in axes:
        count *= lax.axis_size(name)
    return lax.ppermute(x, axis, [(i, to(i)) for i in range(count)])


def z_step(head, step):
    return head // 4 * 4 + (head + step) % 4


def z_by_core(step, i):
    frame, head = i // 8, i % 8
    return frame * 8 + z_step(head, step if frame % 2 == 0 else 4 - step)


swap_core = functools.partial(move, "frame", lambda i: i ^ 1)
out_y = functools.partial(move, "frame", lambda i: (i + (2 if i % 2 == 0 else 6)) % 8)
in_y = functools.partial(move, "frame", lambda i: (i + (6 if i % 2 == 0 else 2)) % 8)
cross_y = functools.partial(move, "frame", lambda i: (i + 4) % 8)
swap_half = functools.partial(move, "spatial", lambda i: i ^ 1)
cross_z = functools.partial(move, "head", lambda i: z_step(i, 2))
out_z = functools.partial(move, ("frame", "head"), functools.partial(z_by_core, 1))
in_z = functools.partial(move, ("frame", "head"), functools.partial(z_by_core, 3))
swap_x = functools.partial(move, "head", lambda i: i ^ 4)


def gather_z(x):
    ahead = out_z(x)
    return [x, ahead, in_z(x), out_z(ahead)]


def shards(tokens, w_qkv, w_out, shift, scale, gate, q_gain, k_gain, band, far_tiles):
    frames_dev, half_tok, model_width = tokens.shape
    n_frames = band.shape[0]
    f = lax.axis_index("frame")
    s = lax.axis_index("spatial")
    g = lax.axis_index("head")
    core, y, z, side = f % 2, f // 2, g % 4, g // 4

    step = jnp.where(core == 0, 1, 3)
    w = jnp.transpose(w_qkv, (1, 0, 2))
    blocks_of_w = [(z + by) % 4 + 4 * to for by in (step, 2, 0) for to in (side, 1 - side)]
    place = jnp.stack([s, core] + blocks_of_w)
    kept, sent, q_home, q_send, w_ahead, w_apart = project(
        place, tokens, w, w_out, scale, shift, q_gain, k_gain
    )
    away = swap_half(sent)
    q_away = swap_half(q_send)
    kept_other, kept_first, kept_second = swap_core(kept), out_y(kept), in_y(kept)
    away_other, away_first, away_second = swap_core(away), out_y(away), in_y(away)
    away_across = cross_y(away)
    ahead = (y + jnp.where(core == 0, 3, 1)) % 4
    behind = (y + jnp.where(core == 0, 1, 3)) % 4
    apart = (y + 2) % 4
    blocks = jnp.stack(
        [
            2 * y + core, 2 * y + 1 - core,
            2 * ahead + core, 2 * behind + core,
            2 * behind + 1 - core, 2 * ahead + 1 - core,
            2 * apart + core, 2 * apart + 1 - core,
        ]
    )
    start = f * frames_dev
    meta = jnp.concatenate(
        [
            s.reshape(1),
            blocks,
            start.reshape(1),
            lax.dynamic_slice_in_dim(band, start, frames_dev, 0),
            lax.dynamic_slice_in_dim(far_tiles, start, frames_dev, 0).reshape(-1),
        ]
    ).astype(jnp.int32)
    kept_first = after(kept_first, kept_second, meta)
    kept_across = out_y(kept_first)
    w_ahead, w_apart = out_z(w_ahead), cross_z(w_apart)
    pieces = [kept, away, kept_other, away_other]
    for kept_piece, away_piece in (
        (kept_first, away_first),
        (kept_second, away_second),
    ):
        pieces += [kept_piece, away_piece]
    for kept_piece, away_piece in (
        (kept_first, away_first),
        (kept_second, away_second),
    ):
        pieces += [swap_core(kept_piece), swap_core(away_piece)]
    pieces += [kept_across, away_across, swap_core(kept_across), swap_core(away_across)]
    home, mid_sums, back = attend(
        meta, q_home, q_away, pieces, [w_ahead, w_apart], n_frames
    )
    w_parts = [w_ahead, swap_core(w_ahead), w_apart, swap_core(w_apart)]
    totals = []
    w_all = assemble(place, w_out, w_parts, home)
    for mixed in combine(place, home, mid_sums, swap_half(back), w_all):
        kept_part, sent_part = output(gather_z(mixed), w_all)
        totals.append(kept_part + swap_x(sent_part).astype(F32))
    return jnp.stack([(total * gate).astype(BF16) for total in totals])


def solution(mesh):
    return jax.shard_map(
        shards,
        mesh=mesh,
        in_specs=(
            P("frame", "spatial", None),
            P(None, None, "head"),
            P("head", None),
            P(),
            P(),
            P("head"),
            P(),
            P(),
            P(),
            P(),
        ),
        out_specs=P("frame", "spatial", "head"),
        check_vma=False,
    )
```

```python
import functools

import jax
import jax.numpy as jnp
from jax import lax
from jax.experimental import pallas as pl
from jax.experimental.pallas import tpu as pltpu
from jax.sharding import PartitionSpec as P

HEAD_DIM = 128
TILE = 128
NORM_EPS = 1e-06
LOG2E = 1.4426950408889634
ANY = pl.BlockSpec(memory_space=pl.ANY)
HBM = pl.BlockSpec(memory_space=pltpu.HBM)
VMEM = pl.BlockSpec(memory_space=pltpu.VMEM)
SMEM = pl.BlockSpec(memory_space=pltpu.SMEM)
F32 = jnp.float32
BF16 = jnp.bfloat16


def vmem(mib):
    return pltpu.CompilerParams(vmem_limit_bytes=mib * 1024 * 1024)


def rows_dot(a, b):
    return lax.dot_general(a, b, (((1,), (1,)), ((), ())), preferred_element_type=F32)


def rms_norm(part, gain):
    squares = jnp.mean(part * part, axis=-1, keepdims=True)
    return (part * lax.rsqrt(squares + NORM_EPS) * gain).astype(BF16)


def split_heads(full, gain_row, first):
    parts = [full[:, h * HEAD_DIM:(h + 1) * HEAD_DIM] for h in range(3)]
    if gain_row is None:
        parts = [part.astype(BF16) for part in parts]
    else:
        parts = [rms_norm(part, gain_row) for part in parts]
    return jnp.where(first, parts[0], parts[2]), parts[1], jnp.where(first, parts[2], parts[0])


LANES = tuple(slice(k * HEAD_DIM, (k + 1) * HEAD_DIM) for k in range(4))
CHUNKS = 4


def project_kernel(
    place_ref, x_ref, w_ref, w_out_ref, scale_ref, shift_ref, qg_ref, kg_ref,
    kept_ref, sent_ref, home_ref, q_sent_ref, ahead_ref, apart_ref,
    n_scr, x_scr, w_scr, o_scr, kept_scr, sent_scr, home_scr, q_sent_scr,
    x_sem, w_sem, o_sem, out_sem,
):
    rows, width = x_scr.shape
    chunk = rows // CHUNKS
    wide = w_ref.shape[2]
    x_copies = [
        pltpu.make_async_copy(
            x_ref.at[pl.ds(i * chunk, chunk)], x_scr.at[pl.ds(i * chunk, chunk)], x_sem.at[i]
        )
        for i in range(CHUNKS)
    ]
    w_copies = [
        pltpu.make_async_copy(w_ref.at[j], w_scr.at[:, pl.ds(at * wide, wide)], w_sem.at[at])
        for at, j in enumerate((1, 2, 0))
    ]
    o_load = pltpu.make_async_copy(w_out_ref, o_scr, o_sem.at[0])
    for copy in x_copies + w_copies[:1]:
        copy.start()
    gain = 1.0 + scale_ref[...]
    shift = shift_ref[...]
    first = place_ref[0] == 0
    spans = [slice(i * rows // 2, (i + 1) * rows // 2) for i in range(2)]

    def normalise(i):
        x_copies[i].wait()

        def one_block(step, carry):
            at = pl.ds(pl.multiple_of(i * chunk + step * 16, 16), 16)
            x = x_scr[at, :].astype(F32)
            centred = x - jnp.mean(x, axis=1, keepdims=True)
            var = jnp.mean(centred * centred, axis=1, keepdims=True)
            n_scr[at, :] = (centred * lax.rsqrt(var + NORM_EPS) * gain + shift).astype(BF16)
            return carry

        lax.fori_loop(0, chunk // 16, one_block, 0, unroll=True)

    for i in range(CHUNKS):
        if i == 1:
            for copy in w_copies[1:] + [o_load]:
                copy.start()
        normalise(i)
    w_copies[0].wait()
    w_copies[1].wait()
    for i, at in enumerate(spans):
        full = jnp.dot(n_scr[at, :], w_scr[:, :2 * wide], preferred_element_type=F32)
        for j, gain_row in ((0, kg_ref[...]), (1, None)):
            own, mid, other = split_heads(full[:, j * wide:(j + 1) * wide], gain_row, first)
            kept_scr[at, LANES[j]] = own
            kept_scr[at, LANES[2 + j]] = mid
            sent_scr[at, LANES[j]] = other
    out_copies = [
        pltpu.make_async_copy(sent_scr, sent_ref, out_sem.at[0]),
        pltpu.make_async_copy(kept_scr, kept_ref, out_sem.at[1]),
        pltpu.make_async_copy(home_scr, home_ref, out_sem.at[2]),
        pltpu.make_async_copy(q_sent_scr, q_sent_ref, out_sem.at[3]),
    ]
    out_copies[0].start()
    out_copies[1].start()
    o_load.wait()
    cols, part = ahead_ref.shape[1] // 2, apart_ref.shape[0]
    half = pl.ds(pl.multiple_of(place_ref[1] * part, 16), part)
    o_copies = []
    for j in range(2):
        ahead = pl.ds(pl.multiple_of(place_ref[2 + j] * cols, TILE), cols)
        apart = pl.ds(pl.multiple_of(place_ref[4 + j] * cols, TILE), cols)
        to = pl.ds(j * cols, cols)
        o_copies += [
            pltpu.make_async_copy(o_scr.at[:, ahead], ahead_ref.at[:, to], o_sem.at[1 + 2 * j]),
            pltpu.make_async_copy(o_scr.at[half, apart], apart_ref.at[:, to], o_sem.at[2 + 2 * j]),
        ]
    for copy in o_copies:
        copy.start()
    w_copies[2].wait()
    for at in spans:
        full = jnp.dot(n_scr[at, :], w_scr[:, 2 * wide:], preferred_element_type=F32)
        own, mid, other = split_heads(full, qg_ref[...], first)
        home_scr[at, LANES[0]] = own
        home_scr[at, LANES[1]] = mid
        q_sent_scr[at, LANES[0]] = other
        q_sent_scr[at, LANES[1]] = mid
    out_copies[2].start()
    out_copies[3].start()
    for copy in out_copies + o_copies:
        copy.wait()


def project(place, tokens, w, w_out, scale, shift, q_gain, k_gain):
    frames, half_tok, width = tokens.shape
    rows = frames * half_tok
    shapes = [(rows, 4 * HEAD_DIM)] + [(rows, 2 * HEAD_DIM)] * 3
    depth, cols = w_out.shape[0], w_out.shape[1] // 4
    blocks = [(depth, cols), (depth // 2, cols)]
    pieces = pl.pallas_call(
        project_kernel,
        out_shape=[jax.ShapeDtypeStruct(shape, BF16) for shape in shapes + blocks],
        in_specs=[SMEM, ANY, ANY, ANY] + [VMEM] * 4,
        out_specs=[ANY] * 6,
        scratch_shapes=[
            pltpu.VMEM((rows, width), BF16),
            pltpu.VMEM((rows, width), BF16),
            pltpu.VMEM((width, 9 * HEAD_DIM), BF16),
            pltpu.VMEM(w_out.shape, BF16),
        ]
        + [pltpu.VMEM(shape, BF16) for shape in shapes]
        + [
            pltpu.SemaphoreType.DMA((CHUNKS,)),
            pltpu.SemaphoreType.DMA((3,)),
            pltpu.SemaphoreType.DMA((5,)),
            pltpu.SemaphoreType.DMA((4,)),
        ],
        compiler_params=vmem(56),
        cost_estimate=pl.CostEstimate(
            flops=2 * rows * width * 9 * HEAD_DIM, bytes_accessed=12_000_000, transcendentals=0
        ),
        name="project",
    )(
        place, tokens.reshape(rows, width), w, w_out,
        scale.reshape(1, -1), shift.reshape(1, -1), q_gain.reshape(1, -1), k_gain.reshape(1, -1),
    )
    return [piece.reshape(frames, half_tok, -1) for piece in pieces[:4]] + list(pieces[4:])


META_BLOCKS = 1
META_FRAME = 9
META_BAND = 10
META_FAR = 12
ONES = slice(2 * HEAD_DIM, 3 * HEAD_DIM)
FACTOR = LOG2E * HEAD_DIM ** (-0.5)


def weights_of(q, keys):
    return jnp.exp2(rows_dot(q, keys) * FACTOR)


def key_copies(meta_ref, blocks, pieces, kvo, kvm, sem):
    half = kvm.shape[1]
    s = meta_ref[0]
    near = pl.ds(pl.multiple_of(s * half, half), half)
    away = pl.ds(pl.multiple_of((1 - s) * half, half), half)
    two = pl.ds(0, 2 * HEAD_DIM)
    copies = []
    for at, block in enumerate(blocks):
        frames = pl.ds(2 * block, 2)
        kept, received = pieces[2 * at], pieces[2 * at + 1]
        copies += [
            pltpu.make_async_copy(kept.at[:, :, two], kvo.at[frames, near, two], sem.at[3 * at]),
            pltpu.make_async_copy(
                kept.at[:, :, pl.ds(2 * HEAD_DIM, 2 * HEAD_DIM)],
                kvm.at[frames, :, two],
                sem.at[3 * at + 1],
            ),
            pltpu.make_async_copy(received, kvo.at[frames, away, two], sem.at[3 * at + 2]),
        ]
    return copies


def query_copies(home_ref, away_ref, q_scr, sem, base):
    half = home_ref.shape[1]
    return [
        pltpu.make_async_copy(home_ref, q_scr.at[:, pl.ds(0, half)], sem.at[base]),
        pltpu.make_async_copy(away_ref, q_scr.at[:, pl.ds(half, half)], sem.at[base + 1]),
    ]


def add_frame(fi, at, q_scr, kvo, kvm, acc_o, acc_m):
    for lanes, kv, acc in (
        (slice(0, HEAD_DIM), kvo, acc_o),
        (slice(HEAD_DIM, 2 * HEAD_DIM), kvm, acc_m),
    ):
        keys = kv[at]
        weights = weights_of(q_scr[fi, :, lanes], keys[:, :HEAD_DIM]).astype(BF16)
        acc[fi] += jnp.dot(weights, keys[:, HEAD_DIM:], preferred_element_type=F32)


def attend_kernel(meta_ref, home_ref, away_ref, *refs):
    pieces = refs[0:16]
    out_ref, mid_ref, ret_ref = refs[18:21]
    q_scr, kvo, kvm, acc_o, acc_m, sem = refs[21:27]
    n_frames, half = kvm.shape[0], kvm.shape[1]
    s = meta_ref[0]
    moves = key_copies(
        meta_ref, [meta_ref[META_BLOCKS + r] for r in range(8)], pieces, kvo, kvm, sem
    )
    near = query_copies(home_ref, away_ref, q_scr, sem, 24) + moves[:6]
    band = moves[15:18]
    rest = moves[6:15] + moves[18:]
    for copy in near + band + rest:
        copy.start()
    kvo[:, :, ONES] = jnp.ones((n_frames, 2 * half, HEAD_DIM), BF16)
    kvm[:, :, ONES] = jnp.ones((n_frames, half, HEAD_DIM), BF16)
    acc_o[...] = jnp.zeros_like(acc_o)
    acc_m[...] = jnp.zeros_like(acc_m)
    eye = lax.broadcasted_iota(jnp.int32, (TILE, TILE), 0) == lax.broadcasted_iota(
        jnp.int32, (TILE, TILE), 1
    )
    start = meta_ref[META_FRAME] // 4 * 4

    def add_frames(fi, low, high):
        def one_frame(kf, carry):
            add_frame(fi, kf, q_scr, kvo, kvm, acc_o, acc_m)
            return carry

        lax.fori_loop(low, high + 1, one_frame, 0)

    spans = []
    for fi in range(2):
        frame = meta_ref[META_FRAME] + fi
        width = meta_ref[META_BAND + fi]
        spans.append((jnp.maximum(frame - width, 0), jnp.minimum(frame + width, n_frames - 1)))
    for copy in near:
        copy.wait()
    for fi, (low, high) in enumerate(spans):
        add_frames(fi, jnp.maximum(low, start), jnp.minimum(high, start + 3))
    for copy in band:
        copy.wait()
    for fi, (low, high) in enumerate(spans):
        add_frames(fi, low, start - 1)
        add_frames(fi, start + 4, high)
    for copy in rest:
        copy.wait()
    for fi in range(2):
        for r in range(2):
            for t in range(2):
                at = slice(r * half + t * TILE, r * half + (t + 1) * TILE)
                tile = 2 * (s ^ r) + t
                base = META_FAR + ((fi * 4 + tile) * 4) * 2
                entries = [(meta_ref[base + 2 * j], meta_ref[base + 2 * j + 1]) for j in range(4)]
                flags = []
                for j in range(4):
                    fresh = jnp.bool_(True)
                    for i in range(j):
                        same = (entries[i][0] == entries[j][0]) & (entries[i][1] == entries[j][1])
                        fresh = fresh & jnp.logical_not(same)
                    flags.append(fresh)
                mid_flags = [fresh & (entry[1] // 2 == s) for fresh, entry in zip(flags, entries)]
                for lanes, kv, acc, shown, tiles in (
                    (slice(0, HEAD_DIM), kvo, acc_o, flags, 4),
                    (slice(HEAD_DIM, 2 * HEAD_DIM), kvm, acc_m, mid_flags, 2),
                ):
                    keys = jnp.concatenate(
                        [
                            kv[kf, pl.ds(pl.multiple_of((kt % tiles) * TILE, TILE), TILE), :]
                            for kf, kt in entries
                        ],
                        axis=0,
                    )
                    weights = weights_of(q_scr[fi, at, lanes], keys[:, :HEAD_DIM])
                    weights = jnp.concatenate(
                        [
                            weights[:, j * TILE:(j + 1) * TILE] * jnp.where(shown[j], 1.0, 0.0)
                            for j in range(4)
                        ],
                        axis=1,
                    ).astype(BF16)
                    acc[fi, at, :] += jnp.dot(
                        weights, keys[:, HEAD_DIM:], preferred_element_type=F32
                    )

        attended = (acc_o[fi, :, :HEAD_DIM] / acc_o[fi, :, HEAD_DIM:]).astype(BF16)
        out_ref[fi * half:(fi + 1) * half, :] = attended[:half]
        ret_ref[fi, :half, :HEAD_DIM] = attended[half:]
        mid_ref[fi] = acc_m[fi, :half, :]
        ret_ref[fi, :half, HEAD_DIM:] = acc_m[fi, half:, :HEAD_DIM].astype(BF16)
        dens = []
        for g in range(2):
            den = acc_m[fi, half + g * TILE:half + (g + 1) * TILE, HEAD_DIM:]
            dens.append(jnp.sum(jnp.where(eye, den, 0.0), axis=0, keepdims=True))
        den = jnp.concatenate(dens, axis=0)
        upper = den.astype(BF16).astype(F32)
        block = jnp.concatenate([upper, den - upper, jnp.zeros((12, TILE), F32)], axis=0)
        ret_ref[fi, half:, :HEAD_DIM] = block.astype(BF16)
        ret_ref[fi, half:, HEAD_DIM:] = jnp.zeros((16, HEAD_DIM), BF16)


def attend(meta, q_home, q_away, pieces, waited, n_frames):
    frames, half, _ = q_home.shape
    return pl.pallas_call(
        attend_kernel,
        out_shape=[
            jax.ShapeDtypeStruct((frames * half, HEAD_DIM), BF16),
            jax.ShapeDtypeStruct((frames, half, 2 * HEAD_DIM), F32),
            jax.ShapeDtypeStruct((frames, half + 16, 2 * HEAD_DIM), BF16),
        ],
        in_specs=[SMEM, HBM, HBM]
        + [HBM if at in (0, 1, 3, 13, 15) else ANY for at in range(len(pieces))]
        + [ANY] * len(waited),
        out_specs=[VMEM] * 3,
        scratch_shapes=[
            pltpu.VMEM((frames, 2 * half, 2 * HEAD_DIM), BF16),
            pltpu.VMEM((n_frames, 2 * half, 3 * HEAD_DIM), BF16),
            pltpu.VMEM((n_frames, half, 3 * HEAD_DIM), BF16),
            pltpu.VMEM((frames, 2 * half, 2 * HEAD_DIM), F32),
            pltpu.VMEM((frames, 2 * half, 2 * HEAD_DIM), F32),
            pltpu.SemaphoreType.DMA((26,)),
        ],
        compiler_params=vmem(58),
        cost_estimate=pl.CostEstimate(
            flops=9_000_000_000, bytes_accessed=8_000_000, transcendentals=5_000_000
        ),
        name="attend",
    )(meta, q_home, q_away, *pieces, *waited)


def combine_kernel(place_ref, home_ref, mid_ref, got_ref, _, out0_ref, out1_ref, home, mid, got, sem):
    half = mid.shape[1]
    copies = [
        pltpu.make_async_copy(source, target, sem.at[k])
        for k, (source, target) in enumerate(
            ((got_ref, got), (mid_ref, mid), (home_ref, home))
        )
    ]
    for copy in copies:
        copy.start()
    s = place_ref[0]
    own_lanes = pl.ds(pl.multiple_of(s * 2 * HEAD_DIM, HEAD_DIM), HEAD_DIM)
    other_lanes = pl.ds(pl.multiple_of((1 - s) * 2 * HEAD_DIM, HEAD_DIM), HEAD_DIM)
    eye = lax.broadcasted_iota(jnp.int32, (TILE, TILE), 0) == lax.broadcasted_iota(
        jnp.int32, (TILE, TILE), 1
    )
    ones = jnp.ones((TILE, TILE), BF16)
    for copy in copies:
        copy.wait()
    for fi, out_ref in enumerate((out0_ref, out1_ref)):
        out_ref[:, own_lanes] = home[fi * half:(fi + 1) * half, :]
        out_ref[:, other_lanes] = got[fi, :half, :HEAD_DIM]
        tail = got[fi, half:, :HEAD_DIM].astype(F32)
        for g in range(2):
            at = slice(g * TILE, (g + 1) * TILE)
            upper = jnp.where(eye, tail[g:g + 1, :], 0.0).astype(BF16)
            lower = jnp.where(eye, tail[2 + g:3 + g, :], 0.0).astype(BF16)
            den = jnp.dot(upper, ones, preferred_element_type=F32) + jnp.dot(
                lower, ones, preferred_element_type=F32
            )
            num = mid[fi, at, :HEAD_DIM] + got[fi, at, HEAD_DIM:].astype(F32)
            out_ref[at, HEAD_DIM:2 * HEAD_DIM] = (num / (mid[fi, at, HEAD_DIM:] + den)).astype(BF16)


def combine(place, home, mid, got, later):
    frames, half, _ = mid.shape
    return pl.pallas_call(
        combine_kernel,
        out_shape=[jax.ShapeDtypeStruct((half, 3 * HEAD_DIM), BF16)] * frames,
        in_specs=[SMEM, ANY, ANY, ANY, ANY],
        out_specs=[VMEM] * frames,
        scratch_shapes=[
            pltpu.VMEM(home.shape, home.dtype),
            pltpu.VMEM(mid.shape, mid.dtype),
            pltpu.VMEM(got.shape, got.dtype),
            pltpu.SemaphoreType.DMA((3,)),
        ],
        compiler_params=vmem(6),
        cost_estimate=pl.CostEstimate(
            flops=50_000_000, bytes_accessed=1_500_000, transcendentals=0
        ),
        name="combine",
    )(place, home, mid, got, later)


def after_kernel(*refs):
    pass


def after(x, *waited):
    return pl.pallas_call(
        after_kernel,
        out_shape=jax.ShapeDtypeStruct(x.shape, x.dtype),
        in_specs=[ANY] * (1 + len(waited)),
        out_specs=ANY,
        input_output_aliases={0: 0},
        compiler_params=vmem(2),
        name="after",
    )(x, *waited)


def assemble_kernel(place_ref, w_out_ref, ahead_ref, behind_ref, apart_ref, swapped_ref, *refs):
    all_ref, w_sem = refs[-2:]
    core = place_ref[1]
    depth, part = ahead_ref.shape[0], apart_ref.shape[0]
    cols = all_ref.shape[1] // 2
    copies = []
    for j in range(2):
        block = pl.ds(pl.multiple_of(place_ref[6 + j] * cols, TILE), cols)
        copies.append(
            pltpu.make_async_copy(
                w_out_ref.at[:, block],
                all_ref.at[pl.ds(0, depth), pl.ds(j * cols, cols)],
                w_sem.at[j],
            )
        )
    for k, (source, base) in enumerate(
        (
            (ahead_ref, depth),
            (behind_ref, 2 * depth),
            (apart_ref, 3 * depth + core * part),
            (swapped_ref, 3 * depth + (1 - core) * part),
        )
    ):
        at = pl.ds(pl.multiple_of(base, 16), source.shape[0])
        copies.append(pltpu.make_async_copy(source, all_ref.at[at], w_sem.at[2 + k]))
    for copy in copies:
        copy.start()
    for copy in copies:
        copy.wait()


def assemble(place, w_out, w_parts, later):
    depth, cols = w_parts[0].shape
    return pl.pallas_call(
        assemble_kernel,
        out_shape=jax.ShapeDtypeStruct((4 * depth, cols), BF16),
        in_specs=[SMEM] + [ANY] * 6,
        out_specs=VMEM,
        scratch_shapes=[pltpu.SemaphoreType.DMA((6,))],
        compiler_params=vmem(8),
        cost_estimate=pl.CostEstimate(flops=0, bytes_accessed=4_000_000, transcendentals=0),
        name="assemble",
    )(place, w_out, *w_parts, later)


def output_kernel(*refs):
    mixed, w_ref = refs[0:8], refs[8]
    kept_ref, sent_ref, h_scr, h_sem = refs[9:13]
    cols = kept_ref.shape[1]
    half, width = mixed[0].shape
    copies = [
        pltpu.make_async_copy(
            mixed[k],
            h_scr.at[pl.ds(k // 4 * half, half), pl.ds(k % 4 * width, width)],
            h_sem.at[k],
        )
        for k in range(8)
    ]
    for copy in copies:
        copy.start()
    for copy in copies:
        copy.wait()
    sent_ref[...] = jnp.dot(
        h_scr[...], w_ref[:, cols:], preferred_element_type=F32
    ).astype(BF16)
    kept_ref[...] = jnp.dot(h_scr[...], w_ref[:, :cols], preferred_element_type=F32)


def output(mixed, w_all):
    rows, width = 2 * mixed[0].shape[0], mixed[0].shape[1]
    cols = w_all.shape[1] // 2
    return pl.pallas_call(
        output_kernel,
        out_shape=[
            jax.ShapeDtypeStruct((rows, cols), F32),
            jax.ShapeDtypeStruct((rows, cols), BF16),
        ],
        in_specs=[ANY] * 8 + [VMEM],
        out_specs=[VMEM] * 2,
        scratch_shapes=[
            pltpu.VMEM((rows, 4 * width), BF16),
            pltpu.SemaphoreType.DMA((8,)),
        ],
        compiler_params=vmem(14),
        cost_estimate=pl.CostEstimate(
            flops=16 * rows * width * cols, bytes_accessed=4_000_000, transcendentals=0
        ),
        name="output",
    )(*mixed, w_all)


def move(axis, to, x):
    axes = axis if isinstance(axis, tuple) else (axis,)
    count = 1
    for name in axes:
        count *= lax.axis_size(name)
    return lax.ppermute(x, axis, [(i, to(i)) for i in range(count)])


def z_step(head, step):
    return head // 4 * 4 + (head + step) % 4


def z_by_core(step, i):
    frame, head = i // 8, i % 8
    return frame * 8 + z_step(head, step if frame % 2 == 0 else 4 - step)


swap_core = functools.partial(move, "frame", lambda i: i ^ 1)
out_y = functools.partial(move, "frame", lambda i: (i + (2 if i % 2 == 0 else 6)) % 8)
in_y = functools.partial(move, "frame", lambda i: (i + (6 if i % 2 == 0 else 2)) % 8)
cross_y = functools.partial(move, "frame", lambda i: (i + 4) % 8)
swap_half = functools.partial(move, "spatial", lambda i: i ^ 1)
cross_z = functools.partial(move, "head", lambda i: z_step(i, 2))
out_z = functools.partial(move, ("frame", "head"), functools.partial(z_by_core, 1))
in_z = functools.partial(move, ("frame", "head"), functools.partial(z_by_core, 3))
swap_x = functools.partial(move, "head", lambda i: i ^ 4)


def gather_z(x):
    ahead = out_z(x)
    return [x, ahead, in_z(x), out_z(ahead)]


def shards(tokens, w_qkv, w_out, shift, scale, gate, q_gain, k_gain, band, far_tiles):
    frames_dev, half_tok, model_width = tokens.shape
    n_frames = band.shape[0]
    f = lax.axis_index("frame")
    s = lax.axis_index("spatial")
    g = lax.axis_index("head")
    core, y, z, side = f % 2, f // 2, g % 4, g // 4

    step = jnp.where(core == 0, 1, 3)
    w = jnp.transpose(w_qkv, (1, 0, 2))
    blocks_of_w = [(z + by) % 4 + 4 * to for by in (step, 2, 0) for to in (side, 1 - side)]
    place = jnp.stack([s, core] + blocks_of_w)
    kept, sent, q_home, q_send, w_ahead, w_apart = project(
        place, tokens, w, w_out, scale, shift, q_gain, k_gain
    )
    away = swap_half(sent)
    q_away = swap_half(q_send)
    kept_other, kept_first, kept_second = swap_core(kept), out_y(kept), in_y(kept)
    away_other, away_first, away_second = swap_core(away), out_y(away), in_y(away)
    away_across = cross_y(away)
    ahead = (y + jnp.where(core == 0, 3, 1)) % 4
    behind = (y + jnp.where(core == 0, 1, 3)) % 4
    apart = (y + 2) % 4
    blocks = jnp.stack(
        [
            2 * y + core, 2 * y + 1 - core,
            2 * ahead + core, 2 * behind + core,
            2 * behind + 1 - core, 2 * ahead + 1 - core,
            2 * apart + core, 2 * apart + 1 - core,
        ]
    )
    start = f * frames_dev
    meta = jnp.concatenate(
        [
            s.reshape(1),
            blocks,
            start.reshape(1),
            lax.dynamic_slice_in_dim(band, start, frames_dev, 0),
            lax.dynamic_slice_in_dim(far_tiles, start, frames_dev, 0).reshape(-1),
        ]
    ).astype(jnp.int32)
    kept_first = after(kept_first, kept_second, meta)
    kept_across = out_y(kept_first)
    w_ahead, w_apart = out_z(w_ahead), cross_z(w_apart)
    pieces = [kept, away, kept_other, away_other]
    for kept_piece, away_piece in (
        (kept_first, away_first),
        (kept_second, away_second),
    ):
        pieces += [kept_piece, away_piece]
    for kept_piece, away_piece in (
        (kept_first, away_first),
        (kept_second, away_second),
    ):
        pieces += [swap_core(kept_piece), swap_core(away_piece)]
    pieces += [kept_across, away_across, swap_core(kept_across), swap_core(away_across)]
    home, mid_sums, back = attend(
        meta, q_home, q_away, pieces, [w_ahead, w_apart], n_frames
    )
    w_parts = [w_ahead, swap_core(w_ahead), w_apart, swap_core(w_apart)]
    w_all = assemble(place, w_out, w_parts, home)
    gathered = []
    for mixed in combine(place, home, mid_sums, swap_half(back), w_all):
        gathered += gather_z(mixed)
    kept_part, sent_part = output(gathered, w_all)
    total = kept_part + swap_x(sent_part).astype(F32)
    return (total * gate).astype(BF16).reshape(frames_dev, half_tok, -1)


def solution(mesh):
    return jax.shard_map(
        shards,
        mesh=mesh,
        in_specs=(
            P("frame", "spatial", None),
            P(None, None, "head"),
            P("head", None),
            P(),
            P(),
            P("head"),
            P(),
            P(),
            P(),
            P(),
        ),
        out_specs=P("frame", "spatial", "head"),
        check_vma=False,
    )
```
